256 devices in a mesh: row: 32 (over x, z), col: 8 (over y, core).
Axes of the slice: x: 4, y: 4, z: 8, core: 2. Of those that a mesh axis runs over, the one named last changes fastest.
Arguments:
- affinity: bfloat16 [131072, 8192], P('row', 'col'), may hold values from -250 to 250
- seed_values: int32 [16], replicated, may hold values from 0 to 1073741823
- sku_ids: int32 [8192], P('col'), may hold values from 0 to 8191, each once
Outputs:
- range_basis: float32 [16, 131072], P(None, ('row', 'col'))
- range_factor: float32 [16, 16], replicated
The draws below stay inside these ranges and needn't reach their ends.
All inputs are finite; a program needn't handle non-finite values.
Results may differ from the reference program's by a relative error of at most 0.0046.
Values may be sent and summed in bfloat16 or wider, within the bound.
No kernel may reach another device: no remote copies, remote signals or barrier semaphores. Data moves between devices by JAX's collectives and lax.ppermute only.
A program may use at most 64 MiB of HBM per device.

```python
import math
import jax
import jax.numpy as jnp
from jax import lax

N = 8192
K = 16
ITERS = 2
ROWS = 131072


def draw_affinity(key, part):
    key_base = jax.random.fold_in(key, 11)
    key_rows = jax.random.fold_in(key, 12)
    key_cols = jax.random.fold_in(key, 13)
    position = jnp.arange(ROWS, dtype=jnp.float32)[:, None] / ROWS
    base = jax.random.normal(key_base, (ROWS, N), jnp.float32)
    trend = jnp.exp(math.log(3.0) * position)
    row_scale = jnp.exp(jax.random.uniform(key_rows, (ROWS, 1), jnp.float32, math.log(0.3), math.log(3.0)))
    col_scale = jnp.exp(jax.random.uniform(key_cols, (1, N), jnp.float32, math.log(0.5), math.log(2.0)))
    return (base * trend * row_scale * col_scale).astype(jnp.bfloat16)


def place_ends(result, key, smallest, top_value):
    place = [jax.random.randint(jax.random.fold_in(key, axis), (), 0, length) for axis, length in enumerate(result.shape)]
    longest = result.shape.index(max(result.shape))
    neighbour = place[:longest] + [(place[longest] + 1) % result.shape[longest]] + place[longest + 1:]
    return result.at[tuple(place)].set(smallest).at[tuple(neighbour)].set(top_value)


def setup_inputs(seed: int = 0) -> dict:
    keys = jax.random.split(jax.random.key(seed), 4)
    return {
        "affinity": draw_affinity(jax.random.fold_in(keys[3], 71), 0),
        "seed_values": place_ends(jax.random.randint(keys[1], (K,), 0, 1073741824), jax.random.fold_in(keys[1], 1), 0, 1073741823).astype(jnp.int32),
        "sku_ids": jax.random.permutation(keys[2], N).astype(jnp.int32),
    }


mix_first = -2048144789
mix_second = -1028477387
golden = -1640531535
salt_value = 1540483477

def shifted(value, amount):
    return lax.shift_right_logical(value, jnp.full(value.shape, amount, jnp.int32))

def scramble(value):
    value = jnp.bitwise_xor(value, shifted(value, 16))
    value = value * jnp.int32(mix_first)
    value = jnp.bitwise_xor(value, shifted(value, 13))
    value = value * jnp.int32(mix_second)
    return jnp.bitwise_xor(value, shifted(value, 16))

def test_matrix(seed_values, sku_ids, total_columns):
    first = scramble(jnp.bitwise_xor(seed_values[:, None], sku_ids[None, :] * jnp.int32(golden)))
    second = scramble(jnp.bitwise_xor(first, jnp.int32(salt_value)))
    uniform_a = (shifted(first, 9) + 1).astype(jnp.float32) / 8388608.0
    uniform_b = (shifted(second, 9) + 1).astype(jnp.float32) / 8388608.0
    gauss = jnp.sqrt(-2.0 * jnp.log(uniform_a)) * jnp.cos(6.283185307179586 * uniform_b)
    return (gauss / math.sqrt(total_columns)).astype(jnp.bfloat16)

def project(left, affinity):
    return lax.dot_general(left.astype(jnp.float32), affinity.astype(jnp.float32), (((1,), (1,)), ((), ())), preferred_element_type=jnp.float32)

def lower_solve(lower, right):
    return lax.linalg.triangular_solve(lower, right, left_side=True, lower=True)

def reference(affinity, seed_values, sku_ids):
    omega = test_matrix(seed_values, sku_ids, N)
    sketch = project(omega, affinity)
    for repeat in range(ITERS + 1):
        gram = jnp.dot(sketch.astype(jnp.float32), sketch.T.astype(jnp.float32), precision=lax.Precision.HIGHEST, preferred_element_type=jnp.float32)
        lower = jnp.linalg.cholesky(gram)
        ortho = lower_solve(lower, sketch)
        if repeat < ITERS:
            back = jnp.dot(ortho.astype(jnp.bfloat16).astype(jnp.float32), affinity.astype(jnp.float32), preferred_element_type=jnp.float32)
            sketch = project(back.astype(jnp.bfloat16), affinity) * (1.0 / math.sqrt(N))
    scale = math.sqrt(ROWS)
    return (ortho * scale, lower.T / scale)
```

```python
import math

import jax
import jax.numpy as jnp
from jax import lax
from jax.sharding import Mesh, PartitionSpec as P

ITERS = 2
K = 16


mix_first = -2048144789
mix_second = -1028477387
golden = -1640531535
salt_value = 1540483477


def shifted(value, amount):
    return lax.shift_right_logical(value, jnp.full(value.shape, amount, jnp.int32))


def scramble(value):
    value = jnp.bitwise_xor(value, shifted(value, 16))
    value = value * jnp.int32(mix_first)
    value = jnp.bitwise_xor(value, shifted(value, 13))
    value = value * jnp.int32(mix_second)
    return jnp.bitwise_xor(value, shifted(value, 16))


def test_matrix(seed_values, sku_ids, total_columns):
    first = scramble(jnp.bitwise_xor(seed_values[:, None], sku_ids[None, :] * jnp.int32(golden)))
    second = scramble(jnp.bitwise_xor(first, jnp.int32(salt_value)))
    uniform_a = (shifted(first, 9) + 1).astype(jnp.float32) / 8388608.0
    uniform_b = (shifted(second, 9) + 1).astype(jnp.float32) / 8388608.0
    gauss = jnp.sqrt(-2.0 * jnp.log(uniform_a)) * jnp.cos(6.283185307179586 * uniform_b)
    return (gauss / math.sqrt(total_columns)).astype(jnp.bfloat16)


def lower_solve(lower, right):
    return lax.linalg.triangular_solve(lower, right, left_side=True, lower=True)


def swap(value, axis, count, offset):
    return lax.ppermute(value, axis, [(i, i ^ offset) for i in range(count)])


def sum_four(value, axis):
    one, two, three = (swap(value, axis, 4, k) for k in (1, 2, 3))
    return (value + two) + (one + three)


def exact_gram(left):
    return lax.dot_general(
        left,
        left,
        (((1,), (1,)), ((), ())),
        precision=lax.Precision.HIGHEST,
        preferred_element_type=jnp.float32,
    )


def body(affinity, seed_values, sku_ids):
    total_columns = sku_ids.shape[0] * 8
    local_rows = affinity.shape[0]
    total_rows = local_rows * 32
    inv_root = 1.0 / math.sqrt(total_columns)
    core = lax.axis_index("core")
    on_first = core == 0

    def project(left):
        return lax.dot_general(
            left, affinity, (((1,), (1,)), ((), ())), preferred_element_type=jnp.float32
        )

    def halves(partial):
        pieces = partial.reshape(K, 4, 2, local_rows // 8)
        first, second = pieces[:, :, 0], pieces[:, :, 1]
        return jnp.where(on_first, first, second), jnp.where(on_first, second, first)

    omega = test_matrix(seed_values, sku_ids, total_columns)
    partial_sketch = project(omega)
    for repeat in range(ITERS + 1):
        own, other = halves(partial_sketch)
        half = own + swap(other, "core", 2, 1)
        half = sum_four(half, "y")
        if repeat < ITERS:
            sibling = swap(half, "core", 2, 1)
            sketch = jnp.stack(
                [jnp.where(on_first, half, sibling), jnp.where(on_first, sibling, half)], axis=2
            ).reshape(K, local_rows)
            gram = exact_gram(sketch)
            high = sketch.astype(jnp.bfloat16)
            low = (sketch - high.astype(jnp.float32)).astype(jnp.bfloat16)
            both = jnp.dot(
                jnp.concatenate([high, low], axis=0), affinity, preferred_element_type=jnp.float32
            )
            back = both[:K] + both[K:]
            packed = jnp.concatenate([back, gram, jnp.zeros((K, 128 - K), jnp.float32)], axis=1)
            packed = sum_four(packed, "x")
            spread = jnp.broadcast_to(packed[None], (8,) + packed.shape)
            packed = jnp.sum(lax.all_to_all(spread, "z", 0, 0), axis=0)
            gram = packed[:, back.shape[1] : back.shape[1] + K]
            lower = jnp.linalg.cholesky(gram)
            back = lower_solve(lower, packed[:, : back.shape[1]])
            partial_sketch = project(back.astype(jnp.bfloat16)) * inv_root
        else:
            gram = exact_gram(half.reshape(K, local_rows // 2))
            gram = gram + swap(gram, "core", 2, 1)
            gram = jnp.pad(gram, ((0, 0), (0, 128 - K)))
            spread = jnp.broadcast_to(gram[None], (32,) + gram.shape)
            gram = jnp.sum(lax.all_to_all(spread, ("x", "z"), 0, 0), axis=0)[:, :K]
            lower = jnp.linalg.cholesky(gram)
            piece = lax.dynamic_index_in_dim(half, lax.axis_index("y"), 1, keepdims=False)
            ortho = lower_solve(lower, piece)
    scale = math.sqrt(total_rows)
    return (ortho * scale, lower.T / scale)


def solution(mesh):
    split = Mesh(mesh.devices.reshape(4, 8, 4, 2), ("x", "z", "y", "core"))
    row, col = ("x", "z"), ("y", "core")
    return jax.shard_map(
        body,
        mesh=split,
        in_specs=(P(row, col), P(), P(col)),
        out_specs=(P(None, row + col), P()),
        check_vma=False,
    )
```

```python
import functools
import math

import jax
import jax.numpy as jnp
from jax import lax
from jax.experimental import pallas as pl
from jax.experimental.pallas import tpu as pltpu
from jax.sharding import Mesh, PartitionSpec as P

ITERS = 2
K = 16
PIECE = 512


mix_first = -2048144789
mix_second = -1028477387
golden = -1640531535
salt_value = 1540483477


def shifted(value, amount):
    return lax.shift_right_logical(value, jnp.full(value.shape, amount, jnp.int32))


def scramble(value):
    value = jnp.bitwise_xor(value, shifted(value, 16))
    value = value * jnp.int32(mix_first)
    value = jnp.bitwise_xor(value, shifted(value, 13))
    value = value * jnp.int32(mix_second)
    return jnp.bitwise_xor(value, shifted(value, 16))


def test_matrix(seed_values, sku_ids, total_columns):
    first = scramble(jnp.bitwise_xor(seed_values[:, None], sku_ids[None, :] * jnp.int32(golden)))
    second = scramble(jnp.bitwise_xor(first, jnp.int32(salt_value)))
    uniform_a = (shifted(first, 9) + 1).astype(jnp.float32) / 8388608.0
    uniform_b = (shifted(second, 9) + 1).astype(jnp.float32) / 8388608.0
    gauss = jnp.sqrt(-2.0 * jnp.log(uniform_a)) * jnp.cos(6.283185307179586 * uniform_b)
    return (gauss / math.sqrt(total_columns)).astype(jnp.bfloat16)


def swap(value, axis, count, offset):
    return lax.ppermute(value, axis, [(i, i ^ offset) for i in range(count)])


def sum_four(value, axis, count):
    one, two, three = (swap(value, axis, count, k) for k in (1, 2, 3))
    return (value + two) + (one + three)


def block_rows(piece, core):
    return pl.ds(pl.multiple_of((2 * piece + core) * PIECE, PIECE), PIECE)


def project_into(left, affinity, own, other, scale):
    core = lax.axis_index("core")
    for target, side in ((other, 1 - core), (own, core)):
        for step in range(4):
            part = lax.dot_general(
                left,
                affinity[block_rows(step, side), :],
                (((1,), (1,)), ((), ())),
                preferred_element_type=jnp.float32,
            )
            if scale is not None:
                part = part * scale
            target[:, step * PIECE : (step + 1) * PIECE] = part


def eliminate(gram, right):
    row = lax.broadcasted_iota(jnp.int32, (K, 128), 0)
    lane = lax.broadcasted_iota(jnp.int32, (K, 128), 1)
    columns = [jnp.broadcast_to(gram[:, k : k + 1], (K, 128)) for k in range(K)]
    lower = jnp.zeros((K, 128), jnp.float32)
    pivots = jnp.ones((K, 128), jnp.float32)
    for k in range(K):
        column = columns[k]
        pivot = jnp.broadcast_to(column[k : k + 1, :], (K, 128))
        factor = column * (1.0 / pivot)
        lower = jnp.where((lane == k) & (row >= k), column / jnp.sqrt(pivot), lower)
        pivots = jnp.where(row == k, pivot, pivots)
        factor = jnp.where(row > k, factor, 0.0)
        for j in range(k + 1, K):
            columns[j] = columns[j] - factor * jnp.broadcast_to(column[j : j + 1, :], (K, 128))
        wide = jnp.tile(factor, (1, right.shape[1] // 128))
        right = right - wide * right[k : k + 1, :]
    root = jnp.sqrt(pivots)
    return lower, right / jnp.tile(root, (1, right.shape[1] // 128))


def first_kernel(omega, affinity, own, other):
    project_into(omega[...], affinity, own, other, None)


def back_kernel(own, sibling, affinity, packed):
    core = lax.axis_index("core")
    both = jnp.zeros((2 * K, affinity.shape[1]), jnp.float32)
    gram = jnp.zeros((3 * K, 3 * K), jnp.float32)
    for source, side in ((own, core), (sibling, 1 - core)):
        for step in range(4):
            value = source[:, step * PIECE : (step + 1) * PIECE]
            high = value.astype(jnp.bfloat16)
            rest = value - high.astype(jnp.float32)
            low = rest.astype(jnp.bfloat16)
            last = (rest - low.astype(jnp.float32)).astype(jnp.bfloat16)
            pair = jnp.concatenate([high, low], axis=0)
            triple = jnp.concatenate([pair, last], axis=0)
            both += jnp.dot(
                pair, affinity[block_rows(step, side), :], preferred_element_type=jnp.float32
            )
            gram += lax.dot_general(
                triple, triple, (((1,), (1,)), ((), ())), preferred_element_type=jnp.float32
            )
    wide = affinity.shape[1]
    packed[:, :wide] = both[:K] + both[K:]
    rows = (gram[2 * K :] + gram[K : 2 * K]) + gram[:K]
    packed[:, wide:] = jnp.zeros((K, 128), jnp.float32)
    packed[:, wide : wide + K] = (rows[:, 2 * K :] + rows[:, K : 2 * K]) + rows[:, :K]


def solve_kernel(mine, theirs, affinity, own, other, *, scale):
    wide = affinity.shape[1]
    total = mine[...] + theirs[...]
    _, back = eliminate(total[:, wide:], total[:, :wide])
    project_into(back.astype(jnp.bfloat16), affinity, own, other, scale)


def last_kernel(grams, half, basis, factor, *, scale):
    gram = jnp.sum(grams[...], axis=0)
    place = pl.multiple_of(lax.axis_index("y") * PIECE, PIECE)
    lower, ortho = eliminate(gram, half[:, pl.ds(place, PIECE)])
    basis[...] = ortho * scale
    factor[...] = lower.T[:K, :] / scale


def call(kernel, outs, *args):
    whole = pl.BlockSpec(memory_space=pltpu.VMEM)
    return pl.pallas_call(
        kernel,
        in_specs=[whole] * len(args),
        out_specs=[whole] * len(outs),
        out_shape=[jax.ShapeDtypeStruct(shape, jnp.float32) for shape in outs],
        compiler_params=pltpu.CompilerParams(vmem_limit_bytes=32 * 1024 * 1024),
    )(*args)


def body(affinity, seed_values, sku_ids):
    local_rows, local_columns = affinity.shape
    total_columns = local_columns * 8
    total_rows = local_rows * 32
    half_shape = (K, local_rows // 2)
    packed_shape = (K, local_columns + 128)

    omega = test_matrix(seed_values, sku_ids, total_columns)
    own, other = call(first_kernel, [half_shape] * 2, omega, affinity)
    for repeat in range(ITERS + 1):
        half = sum_four(own + swap(other, "core", 2, 1), "y", 4)
        if repeat < ITERS:
            sibling = swap(half, "core", 2, 1)
            (packed,) = call(back_kernel, [packed_shape], half, sibling, affinity)
            packed = sum_four(packed, "x", 4)
            packed = sum_four(packed, "z", 8)
            own, other = call(
                functools.partial(solve_kernel, scale=1.0 / math.sqrt(total_columns)),
                [half_shape] * 2,
                packed,
                swap(packed, "z", 8, 6),
                affinity,
            )
        else:
            gram = lax.dot_general(
                half,
                half,
                (((1,), (1,)), ((), ())),
                precision=lax.Precision.HIGHEST,
                preferred_element_type=jnp.float32,
            )
            gram = gram + swap(gram, "core", 2, 1)
            gram = jnp.pad(gram, ((0, 0), (0, 128 - K)))
            spread = jnp.broadcast_to(gram[None], (32,) + gram.shape)
            grams = lax.all_to_all(spread, ("x", "z"), 0, 0)
            basis, factor = call(
                functools.partial(last_kernel, scale=math.sqrt(total_rows)),
                [(K, PIECE), (K, K)],
                grams,
                half,
            )
    return basis, factor


def solution(mesh):
    split = Mesh(mesh.devices.reshape(4, 8, 4, 2), ("x", "z", "y", "core"))
    row, col = ("x", "z"), ("y", "core")
    return jax.shard_map(
        body,
        mesh=split,
        in_specs=(P(row, col), P(), P(col)),
        out_specs=(P(None, row + col), P()),
        check_vma=False,
    )
```

```python
import functools
import math

import jax
import jax.numpy as jnp
from jax import lax
from jax.experimental import pallas as pl
from jax.experimental.pallas import tpu as pltpu
from jax.sharding import Mesh, PartitionSpec as P

ITERS = 2
K = 16
PIECE = 512


mix_first = -2048144789
mix_second = -1028477387
golden = -1640531535
salt_value = 1540483477


def shifted(value, amount):
    return lax.shift_right_logical(value, jnp.full(value.shape, amount, jnp.int32))


def scramble(value):
    value = jnp.bitwise_xor(value, shifted(value, 16))
    value = value * jnp.int32(mix_first)
    value = jnp.bitwise_xor(value, shifted(value, 13))
    value = value * jnp.int32(mix_second)
    return jnp.bitwise_xor(value, shifted(value, 16))


def test_matrix(seeds, sku_ids, total_columns):
    first = scramble(jnp.bitwise_xor(seeds, sku_ids * jnp.int32(golden)))
    second = scramble(jnp.bitwise_xor(first, jnp.int32(salt_value)))
    uniform_a = (shifted(first, 9) + 1).astype(jnp.float32) / 8388608.0
    uniform_b = (shifted(second, 9) + 1).astype(jnp.float32) / 8388608.0
    gauss = jnp.sqrt(-2.0 * jnp.log(uniform_a)) * jnp.cos(6.283185307179586 * uniform_b)
    return (gauss / math.sqrt(total_columns)).astype(jnp.bfloat16)


def swap(value, axis, count, offset):
    return lax.ppermute(value, axis, [(i, i ^ offset) for i in range(count)])


def sum_four(value, axis, count, offsets=(1, 2, 3)):
    one, two, three = (swap(value, axis, count, k) for k in offsets)
    return (value + two) + (one + three)


def block_rows(piece, core):
    return pl.ds(pl.multiple_of((2 * piece + core) * PIECE, PIECE), PIECE)


def span(step):
    return slice(step * PIECE, (step + 1) * PIECE)


def project_piece(left, rows, scale):
    part = lax.dot_general(
        left, rows, (((1,), (1,)), ((), ())), preferred_element_type=jnp.float32
    )
    return part if scale is None else part * scale


def split_bf16(value):
    high = value.astype(jnp.bfloat16)
    rest = value - high.astype(jnp.float32)
    low = rest.astype(jnp.bfloat16)
    last = (rest - low.astype(jnp.float32)).astype(jnp.bfloat16)
    return high, low, last


def triple_gram(parts):
    stacked = jnp.concatenate(parts, axis=0)
    return lax.dot_general(
        stacked, stacked, (((1,), (1,)), ((), ())), preferred_element_type=jnp.float32
    )


def fold_gram(gram):
    rows = (gram[2 * K :] + gram[K : 2 * K]) + gram[:K]
    return (rows[:, 2 * K :] + rows[:, K : 2 * K]) + rows[:, :K]


def eliminate(gram, right):
    row = lax.broadcasted_iota(jnp.int32, (K, 128), 0)
    lane = lax.broadcasted_iota(jnp.int32, (K, 128), 1)
    columns = [jnp.broadcast_to(gram[:, k : k + 1], (K, 128)) for k in range(K)]
    lower = jnp.zeros((K, 128), jnp.float32)
    pivots = jnp.ones((K, 128), jnp.float32)
    for k in range(K):
        column = columns[k]
        pivot = jnp.broadcast_to(column[k : k + 1, :], (K, 128))
        factor = column * (1.0 / pivot)
        lower = jnp.where((lane == k) & (row >= k), column / jnp.sqrt(pivot), lower)
        pivots = jnp.where(row == k, pivot, pivots)
        factor = jnp.where(row > k, factor, 0.0)
        for j in range(k + 1, K):
            columns[j] = columns[j] - factor * jnp.broadcast_to(column[j : j + 1, :], (K, 128))
        wide = jnp.tile(factor, (1, right.shape[1] // 128))
        right = right - wide * right[k : k + 1, :]
    root = jnp.sqrt(pivots)
    return lower, right / jnp.tile(root, (1, right.shape[1] // 128))


def first_kernel(seed_values, sku_ids, affinity, omega, held, other, arrived, *, total_columns):
    core = lax.axis_index("core")
    copies = []
    for side in (1 - core, core):
        for step in range(4):
            place = block_rows(step, side)
            copies.append(
                pltpu.make_async_copy(affinity.at[place], held.at[place], arrived.at[len(copies)])
            )
            copies[-1].start()
    row = lax.broadcasted_iota(jnp.int32, (K, 128), 0)
    seeds = jnp.zeros((K, 128), jnp.int32)
    for k in range(K):
        seeds = jnp.where(row == k, seed_values[k], seeds)
    for start in range(0, sku_ids.shape[1], 128):
        ids = jnp.broadcast_to(sku_ids[:, start : start + 128], (K, 128))
        omega[:, start : start + 128] = test_matrix(seeds, ids, total_columns)
    for step in range(4):
        copies[step].wait()
        rows = held[block_rows(step, 1 - core), :]
        other[:, span(step)] = project_piece(omega[...], rows, None)
    for step in range(4, 8):
        copies[step].wait()


def solve_kernel(mine, theirs, held, left, other, *, scale):
    core = lax.axis_index("core")
    wide = held.shape[1]
    total = mine[...] + theirs[...]
    _, back = eliminate(total[:, wide:], total[:, :wide])
    left[...] = back.astype(jnp.bfloat16)
    for step in range(4):
        rows = held[block_rows(step, 1 - core), :]
        other[:, span(step)] = project_piece(left[...], rows, scale)


def own_kernel(left, held, own, *, scale):
    core = lax.axis_index("core")
    for step in range(4):
        rows = held[block_rows(step, core), :]
        own[:, span(step)] = project_piece(left[...], rows, scale)


def back_sums(half, held, side):
    both = jnp.zeros((2 * K, held.shape[1]), jnp.float32)
    gram = jnp.zeros((3 * K, 3 * K), jnp.float32)
    for step in range(4):
        parts = split_bf16(half[:, span(step)])
        both += jnp.dot(
            jnp.concatenate(parts[:2], axis=0),
            held[block_rows(step, side), :],
            preferred_element_type=jnp.float32,
        )
        gram += triple_gram(parts)
    return both[:K] + both[K:], fold_gram(gram)


def back_own_kernel(half, held, packed):
    wide = held.shape[1]
    back, gram = back_sums(half, held, lax.axis_index("core"))
    packed[:, :wide] = back
    packed[:, wide:] = jnp.zeros((K, 128), jnp.float32)
    packed[:, wide : wide + K] = gram


def back_other_kernel(half, held, before, packed):
    wide = held.shape[1]
    back, gram = back_sums(half, held, 1 - lax.axis_index("core"))
    packed[:, :wide] = before[:, :wide] + back
    packed[:, wide:] = jnp.zeros((K, 128), jnp.float32)
    packed[:, wide : wide + K] = before[:, wide : wide + K] + gram


def gram_kernel(half, packed):
    gram = jnp.zeros((3 * K, 3 * K), jnp.float32)
    for step in range(4):
        gram += triple_gram(split_bf16(half[:, span(step)]))
    gram = fold_gram(gram)
    packed[...] = jnp.zeros_like(packed)
    packed[:, :K] = gram[:8]
    packed[:, K : 2 * K] = gram[8:]


def last_kernel(grams, half, basis, factor, *, scale):
    total = None
    for x in range(4):
        one, two, three, four = (grams[4 * x + k] for k in range(4))
        part = (one + three) + (two + four)
        total = part if total is None else total + part
    gram = jnp.concatenate([total[:, :K], total[:, K : 2 * K]], axis=0)
    place = pl.multiple_of(lax.axis_index("y") * PIECE, PIECE)
    lower, ortho = eliminate(gram, half[:, pl.ds(place, PIECE)])
    basis[...] = ortho * scale
    factor[...] = lower.T[:K, :] / scale


def call(kernel, outs, *args, spaces=None, scratch=(), flops=0):
    whole = pl.BlockSpec(memory_space=pltpu.VMEM)
    return pl.pallas_call(
        kernel,
        in_specs=spaces or [whole] * len(args),
        out_specs=[whole] * len(outs),
        out_shape=[jax.ShapeDtypeStruct(*out) for out in outs],
        scratch_shapes=scratch,
        cost_estimate=pl.CostEstimate(
            flops=flops, bytes_accessed=flops // K, transcendentals=0
        ),
        compiler_params=pltpu.CompilerParams(vmem_limit_bytes=32 * 1024 * 1024),
    )(*args)


def body(affinity, seed_values, sku_ids):
    local_rows, local_columns = affinity.shape
    total_columns = local_columns * 8
    total_rows = local_rows * 32
    f32 = jnp.float32
    half_out = ((K, local_rows // 2), f32)
    left_out = ((K, local_columns), jnp.bfloat16)
    packed_out = ((K, local_columns + 128), f32)
    pass_flops = K * local_rows * local_columns
    z = ("cube", "level")

    left, held, other = call(
        functools.partial(first_kernel, total_columns=total_columns),
        [left_out, (affinity.shape, jnp.bfloat16), half_out],
        seed_values,
        sku_ids.reshape(1, -1),
        pltpu.with_memory_space_constraint(affinity, pltpu.HBM),
        spaces=[
            pl.BlockSpec(memory_space=pltpu.SMEM),
            pl.BlockSpec(memory_space=pltpu.VMEM),
            pl.BlockSpec(memory_space=pltpu.HBM),
        ],
        scratch=[pltpu.SemaphoreType.DMA((8,))],
        flops=pass_flops,
    )
    scale = None
    for repeat in range(ITERS + 1):
        arriving = swap(other, "core", 2, 1)
        (own,) = call(
            functools.partial(own_kernel, scale=scale), [half_out], left, held, flops=pass_flops
        )
        half = sum_four(own + arriving, "y", 4)
        if repeat < ITERS:
            sibling = swap(half, "core", 2, 1)
            (packed,) = call(back_own_kernel, [packed_out], half, held, flops=pass_flops)
            (packed,) = call(
                back_other_kernel, [packed_out], sibling, held, packed, flops=pass_flops
            )
            packed = sum_four(packed, "x", 4)
            packed = sum_four(packed, z, 8)
            scale = 1.0 / math.sqrt(total_columns)
            left, other = call(
                functools.partial(solve_kernel, scale=scale),
                [left_out, half_out],
                packed,
                swap(packed, z, 8, 6),
                held,
                flops=pass_flops,
            )
        else:
            (gram,) = call(gram_kernel, [((8, 128), f32)], half)
            gram = sum_four(gram, z + ("core",), 16, (1, 12, 13))
            spread = jnp.broadcast_to(gram[None], (16,) + gram.shape)
            grams = lax.all_to_all(spread, ("x", "level"), 0, 0)
            basis, factor = call(
                functools.partial(last_kernel, scale=math.sqrt(total_rows)),
                [((K, PIECE), f32), ((K, K), f32)],
                grams,
                half,
            )
    return basis, factor


def solution(mesh):
    names = ("x", "cube", "level", "y", "core")
    split = Mesh(mesh.devices.reshape(4, 2, 4, 4, 2), names)
    row, col = names[:3], names[3:]
    return jax.shard_map(
        body,
        mesh=split,
        in_specs=(P(row, col), P(), P(col)),
        out_specs=(P(None, row + col), P()),
        check_vma=False,
    )
```

```python
import functools
import math

import jax
import jax.numpy as jnp
from jax import lax
from jax.experimental import pallas as pl
from jax.experimental.pallas import tpu as pltpu
from jax.sharding import Mesh, PartitionSpec as P

ITERS = 2
K = 16
PIECE = 512


mix_first = -2048144789
mix_second = -1028477387
golden = -1640531535
salt_value = 1540483477


def shifted(value, amount):
    return lax.shift_right_logical(value, jnp.full(value.shape, amount, jnp.int32))


def scramble(value):
    value = jnp.bitwise_xor(value, shifted(value, 16))
    value = value * jnp.int32(mix_first)
    value = jnp.bitwise_xor(value, shifted(value, 13))
    value = value * jnp.int32(mix_second)
    return jnp.bitwise_xor(value, shifted(value, 16))


def test_matrix(seeds, sku_ids, total_columns):
    first = scramble(jnp.bitwise_xor(seeds, sku_ids * jnp.int32(golden)))
    second = scramble(jnp.bitwise_xor(first, jnp.int32(salt_value)))
    uniform_a = (shifted(first, 9) + 1).astype(jnp.float32) / 8388608.0
    uniform_b = (shifted(second, 9) + 1).astype(jnp.float32) / 8388608.0
    gauss = jnp.sqrt(-2.0 * jnp.log(uniform_a)) * jnp.cos(6.283185307179586 * uniform_b)
    return (gauss / math.sqrt(total_columns)).astype(jnp.bfloat16)


def swap(value, axis, count, offset):
    return lax.ppermute(value, axis, [(i, i ^ offset) for i in range(count)])


def sum_four(value, axis, count, offsets=(1, 2, 3)):
    one, two, three = (swap(value, axis, count, k) for k in offsets)
    return (value + two) + (one + three)


def span(step):
    return slice(step * PIECE, (step + 1) * PIECE)


def project_piece(left, rows, scale):
    part = lax.dot_general(
        left, rows, (((1,), (1,)), ((), ())), preferred_element_type=jnp.float32
    )
    return part if scale is None else part * scale


def split_bf16(value):
    high = value.astype(jnp.bfloat16)
    rest = value - high.astype(jnp.float32)
    low = rest.astype(jnp.bfloat16)
    last = (rest - low.astype(jnp.float32)).astype(jnp.bfloat16)
    return high, low, last


def triple_gram(parts):
    stacked = jnp.concatenate(parts, axis=0)
    return lax.dot_general(
        stacked, stacked, (((1,), (1,)), ((), ())), preferred_element_type=jnp.float32
    )


def fold_gram(gram):
    rows = (gram[2 * K :] + gram[K : 2 * K]) + gram[:K]
    return (rows[:, 2 * K :] + rows[:, K : 2 * K]) + rows[:, :K]


def eliminate(gram, right):
    row = lax.broadcasted_iota(jnp.int32, (K, 128), 0)
    lane = lax.broadcasted_iota(jnp.int32, (K, 128), 1)
    columns = [jnp.broadcast_to(gram[:, k : k + 1], (K, 128)) for k in range(K)]
    lower = jnp.zeros((K, 128), jnp.float32)
    pivots = jnp.ones((K, 128), jnp.float32)
    for k in range(K):
        column = columns[k]
        pivot = jnp.broadcast_to(column[k : k + 1, :], (K, 128))
        factor = column * (1.0 / pivot)
        lower = jnp.where((lane == k) & (row >= k), column / jnp.sqrt(pivot), lower)
        pivots = jnp.where(row == k, pivot, pivots)
        factor = jnp.where(row > k, factor, 0.0)
        for j in range(k + 1, K):
            columns[j] = columns[j] - factor * jnp.broadcast_to(column[j : j + 1, :], (K, 128))
        wide = jnp.tile(factor, (1, right.shape[1] // 128))
        right = right - wide * right[k : k + 1, :]
    root = jnp.sqrt(pivots)
    return lower, right / jnp.tile(root, (1, right.shape[1] // 128))


def load_half(affinity, held, arrived, side):
    copies = []
    for step in range(4):
        place = pl.multiple_of((2 * step + side) * PIECE, PIECE)
        copies.append(
            pltpu.make_async_copy(
                affinity.at[pl.ds(place, PIECE)], held.at[span(step)], arrived.at[step]
            )
        )
        copies[-1].start()
    return copies


def project_half(left, held, target, scale, copies=None):
    for step in range(4):
        if copies is not None:
            copies[step].wait()
        target[:, span(step)] = project_piece(left[...], held[span(step), :], scale)


def first_kernel(
    seed_values, sku_ids, affinity, left, held, other, seeds_here, ids_here, arrived, *, columns
):
    small = [
        pltpu.make_async_copy(seed_values, seeds_here, arrived.at[4]),
        pltpu.make_async_copy(sku_ids, ids_here, arrived.at[5]),
    ]
    for copy in small:
        copy.start()
    copies = load_half(affinity, held, arrived, 1 - lax.axis_index("core"))
    for copy in small:
        copy.wait()
    row = lax.broadcasted_iota(jnp.int32, (K, 128), 0)
    seeds = jnp.zeros((K, 128), jnp.int32)
    for k in range(K):
        seeds = jnp.where(row == k, seeds_here[k], seeds)
    for start in range(0, ids_here.shape[1], 128):
        ids = jnp.broadcast_to(ids_here[:, start : start + 128], (K, 128))
        left[:, start : start + 128] = test_matrix(seeds, ids, columns)
    project_half(left, held, other, None, copies)


def first_own_kernel(left, affinity, held, own, arrived):
    copies = load_half(affinity, held, arrived, lax.axis_index("core"))
    project_half(left, held, own, None, copies)


def solve_kernel(mine, theirs, held, left, other, *, scale):
    wide = held.shape[1]
    total = mine[...] + theirs[...]
    _, back = eliminate(total[:, wide:], total[:, :wide])
    left[...] = back.astype(jnp.bfloat16)
    project_half(left, held, other, scale)


def own_kernel(left, held, own, *, scale):
    project_half(left, held, own, scale)


def back_sums(half, held):
    both = jnp.zeros((2 * K, held.shape[1]), jnp.float32)
    gram = jnp.zeros((3 * K, 3 * K), jnp.float32)
    for step in range(4):
        parts = split_bf16(half[:, span(step)])
        both += jnp.dot(
            jnp.concatenate(parts[:2], axis=0),
            held[span(step), :],
            preferred_element_type=jnp.float32,
        )
        gram += triple_gram(parts)
    return both[:K] + both[K:], fold_gram(gram)


def back_own_kernel(half, held, packed):
    wide = held.shape[1]
    back, gram = back_sums(half, held)
    packed[:, :wide] = back
    packed[:, wide:] = jnp.zeros((K, 128), jnp.float32)
    packed[:, wide : wide + K] = gram


def back_other_kernel(half, held, before, packed):
    wide = held.shape[1]
    back, gram = back_sums(half, held)
    packed[:, :wide] = before[:, :wide] + back
    packed[:, wide:] = jnp.zeros((K, 128), jnp.float32)
    packed[:, wide : wide + K] = before[:, wide : wide + K] + gram


def gram_kernel(half, packed):
    gram = jnp.zeros((3 * K, 3 * K), jnp.float32)
    for step in range(4):
        gram += triple_gram(split_bf16(half[:, span(step)]))
    gram = fold_gram(gram)
    packed[...] = jnp.zeros_like(packed)
    packed[:, :K] = gram[:8]
    packed[:, K : 2 * K] = gram[8:]


def last_kernel(grams, half, basis, factor, *, scale):
    total = None
    for x in range(4):
        one, two, three, four = (grams[4 * x + k] for k in range(4))
        part = (one + three) + (two + four)
        total = part if total is None else total + part
    gram = jnp.concatenate([total[:, :K], total[:, K : 2 * K]], axis=0)
    place = pl.multiple_of(lax.axis_index("y") * PIECE, PIECE)
    lower, ortho = eliminate(gram, half[:, pl.ds(place, PIECE)])
    basis[...] = ortho * scale
    factor[...] = lower.T[:K, :] / scale


def call(kernel, outs, *args, spaces=None, scratch=(), flops=0):
    whole = pl.BlockSpec(memory_space=pltpu.VMEM)
    return pl.pallas_call(
        kernel,
        in_specs=spaces or [whole] * len(args),
        out_specs=[whole] * len(outs),
        out_shape=[jax.ShapeDtypeStruct(*out) for out in outs],
        scratch_shapes=scratch,
        cost_estimate=pl.CostEstimate(
            flops=flops, bytes_accessed=flops // K, transcendentals=0
        ),
        compiler_params=pltpu.CompilerParams(vmem_limit_bytes=32 * 1024 * 1024),
    )(*args)


def body(affinity, seed_values, sku_ids):
    local_rows, local_columns = affinity.shape
    total_columns = local_columns * 8
    total_rows = local_rows * 32
    f32 = jnp.float32
    half_out = ((K, local_rows // 2), f32)
    left_out = ((K, local_columns), jnp.bfloat16)
    packed_out = ((K, local_columns + 128), f32)
    pass_flops = K * local_rows * local_columns
    z = ("cube", "level")

    held_out = ((local_rows // 2, local_columns), jnp.bfloat16)
    far = pl.BlockSpec(memory_space=pltpu.HBM)
    near = pl.BlockSpec(memory_space=pltpu.VMEM)
    affinity, seed_values, sku_ids = (
        pltpu.with_memory_space_constraint(value, pltpu.HBM)
        for value in (affinity, seed_values, sku_ids.reshape(1, -1))
    )

    left, held_other, other = call(
        functools.partial(first_kernel, columns=total_columns),
        [left_out, held_out, half_out],
        seed_values,
        sku_ids,
        affinity,
        spaces=[far, far, far],
        scratch=[
            pltpu.SMEM(seed_values.shape, jnp.int32),
            pltpu.VMEM(sku_ids.shape, jnp.int32),
            pltpu.SemaphoreType.DMA((6,)),
        ],
        flops=pass_flops,
    )
    scale = 1.0 / math.sqrt(total_columns)
    for repeat in range(ITERS + 1):
        arriving = swap(other, "core", 2, 1)
        if repeat == 0:
            held_own, own = call(
                first_own_kernel,
                [held_out, half_out],
                left,
                affinity,
                spaces=[near, far],
                scratch=[pltpu.SemaphoreType.DMA((4,))],
                flops=pass_flops,
            )
        else:
            (own,) = call(
                functools.partial(own_kernel, scale=scale),
                [half_out],
                left,
                held_own,
                flops=pass_flops,
            )
        half = sum_four(own + arriving, "y", 4)
        if repeat < ITERS:
            sibling = swap(half, "core", 2, 1)
            (packed,) = call(back_own_kernel, [packed_out], half, held_own, flops=pass_flops)
            (packed,) = call(
                back_other_kernel, [packed_out], sibling, held_other, packed, flops=pass_flops
            )
            packed = sum_four(packed, "x", 4)
            packed = sum_four(packed, z, 8)
            left, other = call(
                functools.partial(solve_kernel, scale=scale),
                [left_out, half_out],
                packed,
                swap(packed, z, 8, 6),
                held_other,
                flops=pass_flops,
            )
        else:
            (gram,) = call(gram_kernel, [((8, 128), f32)], half)
            gram = sum_four(gram, z + ("core",), 16, (1, 12, 13))
            spread = jnp.broadcast_to(gram[None], (16,) + gram.shape)
            grams = lax.all_to_all(spread, ("x", "level"), 0, 0)
            basis, factor = call(
                functools.partial(last_kernel, scale=math.sqrt(total_rows)),
                [((K, PIECE), f32), ((K, K), f32)],
                grams,
                half,
            )
    return basis, factor


def solution(mesh):
    names = ("x", "cube", "level", "y", "core")
    split = Mesh(mesh.devices.reshape(4, 2, 4, 4, 2), names)
    row, col = names[:3], names[3:]
    return jax.shard_map(
        body,
        mesh=split,
        in_specs=(P(row, col), P(), P(col)),
        out_specs=(P(None, row + col), P()),
        check_vma=False,
    )
```

```python
import functools
import math

import jax
import jax.numpy as jnp
from jax import lax
from jax.experimental import pallas as pl
from jax.experimental.pallas import tpu as pltpu
from jax.sharding import Mesh, PartitionSpec as P

ITERS = 2
K = 16
PIECE = 512


mix_first = -2048144789
mix_second = -1028477387
golden = -1640531535
salt_value = 1540483477


def shifted(value, amount):
    return lax.shift_right_logical(value, jnp.full(value.shape, amount, jnp.int32))


def scramble(value):
    value = jnp.bitwise_xor(value, shifted(value, 16))
    value = value * jnp.int32(mix_first)
    value = jnp.bitwise_xor(value, shifted(value, 13))
    value = value * jnp.int32(mix_second)
    return jnp.bitwise_xor(value, shifted(value, 16))


def test_matrix(seeds, sku_ids, total_columns):
    first = scramble(jnp.bitwise_xor(seeds, sku_ids * jnp.int32(golden)))
    second = scramble(jnp.bitwise_xor(first, jnp.int32(salt_value)))
    uniform_a = (shifted(first, 9) + 1).astype(jnp.float32) / 8388608.0
    uniform_b = (shifted(second, 9) + 1).astype(jnp.float32) / 8388608.0
    gauss = jnp.sqrt(-2.0 * jnp.log(uniform_a)) * jnp.cos(6.283185307179586 * uniform_b)
    return (gauss / math.sqrt(total_columns)).astype(jnp.bfloat16)


def swap(value, axis, count, offset):
    return lax.ppermute(value, axis, [(i, i ^ offset) for i in range(count)])


def sum_four(value, axis, count, offsets=(1, 2, 3)):
    one, two, three = (swap(value, axis, count, k) for k in offsets)
    return (value + two) + (one + three)


def sum_crossed(value, axes, first, second):
    def swap_by_core(k):
        pairs = [(i, i ^ ((first * k) if i % 2 == 0 else (second * k))) for i in range(64)]
        return lax.ppermute(value, axes, pairs)

    one, two, three = (swap_by_core(k) for k in (1, 2, 3))
    return (value + two) + (one + three)


def span(step):
    return slice(step * PIECE, (step + 1) * PIECE)


def project_piece(left, rows, scale):
    part = lax.dot_general(
        left, rows, (((1,), (1,)), ((), ())), preferred_element_type=jnp.float32
    )
    return part if scale is None else part * scale


def split_bf16(value):
    high = value.astype(jnp.bfloat16)
    rest = value - high.astype(jnp.float32)
    low = rest.astype(jnp.bfloat16)
    last = (rest - low.astype(jnp.float32)).astype(jnp.bfloat16)
    return high, low, last


def triple_gram(parts):
    stacked = jnp.concatenate(parts, axis=0)
    return lax.dot_general(
        stacked, stacked, (((1,), (1,)), ((), ())), preferred_element_type=jnp.float32
    )


def fold_gram(gram):
    rows = (gram[2 * K :] + gram[K : 2 * K]) + gram[:K]
    return (rows[:, 2 * K :] + rows[:, K : 2 * K]) + rows[:, :K]


def eliminate(gram, right):
    row = lax.broadcasted_iota(jnp.int32, (K, 128), 0)
    lane = lax.broadcasted_iota(jnp.int32, (K, 128), 1)
    columns = [jnp.broadcast_to(gram[:, k : k + 1], (K, 128)) for k in range(K)]
    lower = jnp.zeros((K, 128), jnp.float32)
    pivots = jnp.ones((K, 128), jnp.float32)
    for k in range(K):
        column = columns[k]
        pivot = jnp.broadcast_to(column[k : k + 1, :], (K, 128))
        factor = column * (1.0 / pivot)
        lower = jnp.where((lane == k) & (row >= k), column / jnp.sqrt(pivot), lower)
        pivots = jnp.where(row == k, pivot, pivots)
        factor = jnp.where(row > k, factor, 0.0)
        for j in range(k + 1, K):
            columns[j] = columns[j] - factor * jnp.broadcast_to(column[j : j + 1, :], (K, 128))
        wide = jnp.tile(factor, (1, right.shape[1] // 128))
        right = right - wide * right[k : k + 1, :]
    root = jnp.sqrt(pivots)
    return lower, right / jnp.tile(root, (1, right.shape[1] // 128))


def load_pieces(affinity, held, arrived, side, steps):
    copies = []
    for slot, step in enumerate(steps):
        place = pl.multiple_of((2 * step + side) * PIECE, PIECE)
        copies.append(
            pltpu.make_async_copy(
                affinity.at[pl.ds(place, PIECE)], held.at[span(slot)], arrived.at[slot]
            )
        )
        copies[-1].start()
    return copies


def pieces(*helds):
    return [(held, slot) for held in helds for slot in range(held.shape[0] // PIECE)]


def project_half(left, helds, target, scale, copies=None):
    for step, (held, slot) in enumerate(pieces(*helds)):
        if copies is not None:
            copies[step].wait()
        target[:, span(step)] = project_piece(left[...], held[span(slot), :], scale)


def first_kernel(
    seed_values,
    sku_ids,
    affinity,
    left,
    held_other,
    held_own,
    other,
    seeds_here,
    ids_here,
    small_arrived,
    other_arrived,
    own_arrived,
    *,
    columns,
):
    core = lax.axis_index("core")
    small = [
        pltpu.make_async_copy(seed_values, seeds_here, small_arrived.at[0]),
        pltpu.make_async_copy(sku_ids, ids_here, small_arrived.at[1]),
    ]
    for copy in small:
        copy.start()
    copies = load_pieces(affinity, held_other, other_arrived, 1 - core, range(4))
    ahead = load_pieces(affinity, held_own, own_arrived, core, range(3))
    for copy in small:
        copy.wait()
    row = lax.broadcasted_iota(jnp.int32, (K, 128), 0)
    seeds = jnp.zeros((K, 128), jnp.int32)
    for k in range(K):
        seeds = jnp.where(row == k, seeds_here[k], seeds)
    for start in range(0, ids_here.shape[1], 128):
        ids = jnp.broadcast_to(ids_here[:, start : start + 128], (K, 128))
        left[:, start : start + 128] = test_matrix(seeds, ids, columns)
    project_half(left, [held_other], other, None, copies)
    for copy in ahead:
        copy.wait()


def first_own_kernel(left, held_own, affinity, held_last, own, arrived):
    copies = load_pieces(affinity, held_last, arrived, lax.axis_index("core"), [3])
    project_half(left, [held_own], own, None)
    copies[0].wait()
    own[:, span(3)] = project_piece(left[...], held_last[...], None)


def solve_kernel(mine, theirs, held, left, other, *, scale):
    wide = held.shape[1]
    total = mine[...] + theirs[...]
    _, back = eliminate(total[:, wide:], total[:, :wide])
    left[...] = back.astype(jnp.bfloat16)
    project_half(left, [held], other, scale)


def own_kernel(left, held_own, held_last, own, *, scale):
    project_half(left, [held_own, held_last], own, scale)


def back_sums(half, *helds):
    both = jnp.zeros((2 * K, helds[0].shape[1]), jnp.float32)
    gram = jnp.zeros((3 * K, 3 * K), jnp.float32)
    for step, (held, slot) in enumerate(pieces(*helds)):
        parts = split_bf16(half[:, span(step)])
        both += jnp.dot(
            jnp.concatenate(parts[:2], axis=0),
            held[span(slot), :],
            preferred_element_type=jnp.float32,
        )
        gram += triple_gram(parts)
    return both[:K] + both[K:], fold_gram(gram)


def back_own_kernel(half, held_own, held_last, packed):
    wide = held_own.shape[1]
    back, gram = back_sums(half, held_own, held_last)
    packed[:, :wide] = back
    packed[:, wide:] = jnp.zeros((K, 128), jnp.float32)
    packed[:, wide : wide + K] = gram


def back_other_kernel(half, held, before, packed):
    wide = held.shape[1]
    back, gram = back_sums(half, held)
    packed[:, :wide] = before[:, :wide] + back
    packed[:, wide:] = jnp.zeros((K, 128), jnp.float32)
    packed[:, wide : wide + K] = before[:, wide : wide + K] + gram


def gram_kernel(half, packed):
    gram = jnp.zeros((3 * K, 3 * K), jnp.float32)
    for step in range(4):
        gram += triple_gram(split_bf16(half[:, span(step)]))
    gram = fold_gram(gram)
    packed[...] = jnp.zeros_like(packed)
    packed[:, :K] = gram[:8]
    packed[:, K : 2 * K] = gram[8:]


def last_kernel(grams, half, basis, factor, *, scale):
    total = None
    for x in range(4):
        one, two, three, four = (grams[4 * x + k] for k in range(4))
        part = (one + three) + (two + four)
        total = part if total is None else total + part
    gram = jnp.concatenate([total[:, :K], total[:, K : 2 * K]], axis=0)
    place = pl.multiple_of(lax.axis_index("y") * PIECE, PIECE)
    lower, ortho = eliminate(gram, half[:, pl.ds(place, PIECE)])
    basis[...] = ortho * scale
    factor[...] = lower.T[:K, :] / scale


def call(kernel, outs, *args, spaces=None, scratch=(), flops=0):
    whole = pl.BlockSpec(memory_space=pltpu.VMEM)
    return pl.pallas_call(
        kernel,
        in_specs=spaces or [whole] * len(args),
        out_specs=[whole] * len(outs),
        out_shape=[jax.ShapeDtypeStruct(*out) for out in outs],
        scratch_shapes=scratch,
        cost_estimate=pl.CostEstimate(
            flops=flops, bytes_accessed=flops // K, transcendentals=0
        ),
        compiler_params=pltpu.CompilerParams(vmem_limit_bytes=32 * 1024 * 1024),
    )(*args)


def body(affinity, seed_values, sku_ids):
    local_rows, local_columns = affinity.shape
    total_columns = local_columns * 8
    total_rows = local_rows * 32
    f32 = jnp.float32
    half_out = ((K, local_rows // 2), f32)
    left_out = ((K, local_columns), jnp.bfloat16)
    packed_out = ((K, local_columns + 128), f32)
    pass_flops = K * local_rows * local_columns
    z = ("cube", "level")
    chips = ("x", "cube", "level", "core")

    held_out, ahead_out, last_out = (
        ((count * PIECE, local_columns), jnp.bfloat16) for count in (4, 3, 1)
    )
    far = pl.BlockSpec(memory_space=pltpu.HBM)
    near = pl.BlockSpec(memory_space=pltpu.VMEM)
    affinity, seed_values, sku_ids = (
        pltpu.with_memory_space_constraint(value, pltpu.HBM)
        for value in (affinity, seed_values, sku_ids.reshape(1, -1))
    )

    left, held_other, held_own, other = call(
        functools.partial(first_kernel, columns=total_columns),
        [left_out, held_out, ahead_out, half_out],
        seed_values,
        sku_ids,
        affinity,
        spaces=[far, far, far],
        scratch=[
            pltpu.SMEM(seed_values.shape, jnp.int32),
            pltpu.VMEM(sku_ids.shape, jnp.int32),
            pltpu.SemaphoreType.DMA((2,)),
            pltpu.SemaphoreType.DMA((4,)),
            pltpu.SemaphoreType.DMA((3,)),
        ],
        flops=pass_flops,
    )
    scale = 1.0 / math.sqrt(total_columns)
    for repeat in range(ITERS + 1):
        arriving = swap(other, "core", 2, 1)
        if repeat == 0:
            held_last, own = call(
                first_own_kernel,
                [last_out, half_out],
                left,
                held_own,
                affinity,
                spaces=[near, near, far],
                scratch=[pltpu.SemaphoreType.DMA((1,))],
                flops=pass_flops,
            )
        else:
            (own,) = call(
                functools.partial(own_kernel, scale=scale),
                [half_out],
                left,
                held_own,
                held_last,
                flops=pass_flops,
            )
        half = sum_four(own + arriving, "y", 4)
        if repeat < ITERS:
            sibling = swap(half, "core", 2, 1)
            (packed,) = call(
                back_own_kernel, [packed_out], half, held_own, held_last, flops=pass_flops
            )
            (packed,) = call(
                back_other_kernel, [packed_out], sibling, held_other, packed, flops=pass_flops
            )
            packed = sum_crossed(packed, chips, 16, 2)
            packed = sum_crossed(packed, chips, 2, 16)
            left, other = call(
                functools.partial(solve_kernel, scale=scale),
                [left_out, half_out],
                packed,
                swap(packed, z, 8, 6),
                held_other,
                flops=pass_flops,
            )
        else:
            (gram,) = call(gram_kernel, [((8, 128), f32)], half)
            gram = sum_four(gram, z + ("core",), 16, (1, 12, 13))
            spread = jnp.broadcast_to(gram[None], (16,) + gram.shape)
            grams = lax.all_to_all(spread, ("x", "level"), 0, 0)
            basis, factor = call(
                functools.partial(last_kernel, scale=math.sqrt(total_rows)),
                [((K, PIECE), f32), ((K, K), f32)],
                grams,
                half,
            )
    return basis, factor


def solution(mesh):
    names = ("x", "cube", "level", "y", "core")
    split = Mesh(mesh.devices.reshape(4, 2, 4, 4, 2), names)
    row, col = names[:3], names[3:]
    return jax.shard_map(
        body,
        mesh=split,
        in_specs=(P(row, col), P(), P(col)),
        out_specs=(P(None, row + col), P()),
        check_vma=False,
    )
```

```python
import functools
import math

import jax
import jax.numpy as jnp
from jax import lax
from jax.experimental import pallas as pl
from jax.experimental.pallas import tpu as pltpu
from jax.sharding import Mesh, PartitionSpec as P

ITERS = 2
K = 16
PIECE = 512


mix_first = -2048144789
mix_second = -1028477387
golden = -1640531535
salt_value = 1540483477


def shifted(value, amount):
    return lax.shift_right_logical(value, jnp.full(value.shape, amount, jnp.int32))


def scramble(value):
    value = jnp.bitwise_xor(value, shifted(value, 16))
    value = value * jnp.int32(mix_first)
    value = jnp.bitwise_xor(value, shifted(value, 13))
    value = value * jnp.int32(mix_second)
    return jnp.bitwise_xor(value, shifted(value, 16))


def test_matrix(seeds, sku_ids, total_columns):
    first = scramble(jnp.bitwise_xor(seeds, sku_ids * jnp.int32(golden)))
    second = scramble(jnp.bitwise_xor(first, jnp.int32(salt_value)))
    uniform_a = (shifted(first, 9) + 1).astype(jnp.float32) / 8388608.0
    uniform_b = (shifted(second, 9) + 1).astype(jnp.float32) / 8388608.0
    gauss = jnp.sqrt(-2.0 * jnp.log(uniform_a)) * jnp.cos(6.283185307179586 * uniform_b)
    return (gauss / math.sqrt(total_columns)).astype(jnp.bfloat16)


def swap(value, axis, count, offset):
    return lax.ppermute(value, axis, [(i, i ^ offset) for i in range(count)])


def sum_four(value, axis, count, offsets=(2, 1, 3)):
    one, two, three = (swap(value, axis, count, k) for k in offsets)
    return (value + two) + (one + three)


def span(step):
    return slice(step * PIECE, (step + 1) * PIECE)


def project_piece(left, rows, scale):
    part = lax.dot_general(
        left, rows, (((1,), (1,)), ((), ())), preferred_element_type=jnp.float32
    )
    return part if scale is None else part * scale


def split_bf16(value):
    high = value.astype(jnp.bfloat16)
    rest = value - high.astype(jnp.float32)
    low = rest.astype(jnp.bfloat16)
    last = (rest - low.astype(jnp.float32)).astype(jnp.bfloat16)
    return high, low, last


def triple_gram(parts):
    stacked = jnp.concatenate(parts, axis=0)
    return lax.dot_general(
        stacked, stacked, (((1,), (1,)), ((), ())), preferred_element_type=jnp.float32
    )


def fold_gram(gram):
    rows = (gram[2 * K :] + gram[K : 2 * K]) + gram[:K]
    return (rows[:, 2 * K :] + rows[:, K : 2 * K]) + rows[:, :K]


def eliminate(gram, right):
    row = lax.broadcasted_iota(jnp.int32, (K, 128), 0)
    lane = lax.broadcasted_iota(jnp.int32, (K, 128), 1)
    columns = [jnp.broadcast_to(gram[:, k : k + 1], (K, 128)) for k in range(K)]
    lower = jnp.zeros((K, 128), jnp.float32)
    pivots = jnp.ones((K, 128), jnp.float32)
    for k in range(K):
        column = columns[k]
        pivot = jnp.broadcast_to(column[k : k + 1, :], (K, 128))
        factor = column * (1.0 / pivot)
        lower = jnp.where((lane == k) & (row >= k), column / jnp.sqrt(pivot), lower)
        pivots = jnp.where(row == k, pivot, pivots)
        factor = jnp.where(row > k, factor, 0.0)
        for j in range(k + 1, K):
            columns[j] = columns[j] - factor * jnp.broadcast_to(column[j : j + 1, :], (K, 128))
        wide = jnp.tile(factor, (1, right.shape[1] // 128))
        right = right - wide * right[k : k + 1, :]
    root = jnp.sqrt(pivots)
    return lower, right / jnp.tile(root, (1, right.shape[1] // 128))


def load_half(affinity, held, arrived, side):
    copies = []
    for step in range(4):
        place = pl.multiple_of((2 * step + side) * PIECE, PIECE)
        copies.append(
            pltpu.make_async_copy(
                affinity.at[pl.ds(place, PIECE)], held.at[span(step)], arrived.at[step]
            )
        )
        copies[-1].start()
    return copies


def project_half(left, held, target, scale, copies=None):
    for step in range(4):
        if copies is not None:
            copies[step].wait()
        target[:, span(step)] = project_piece(left[...], held[span(step), :], scale)


def first_kernel(
    seed_values, sku_ids, affinity, left, held, other, seeds_here, ids_here, arrived, *, columns
):
    small = [
        pltpu.make_async_copy(seed_values, seeds_here, arrived.at[4]),
        pltpu.make_async_copy(sku_ids, ids_here, arrived.at[5]),
    ]
    for copy in small:
        copy.start()
    copies = load_half(affinity, held, arrived, 1 - lax.axis_index("core"))
    for copy in small:
        copy.wait()
    row = lax.broadcasted_iota(jnp.int32, (K, 128), 0)
    seeds = jnp.zeros((K, 128), jnp.int32)
    for k in range(K):
        seeds = jnp.where(row == k, seeds_here[k], seeds)
    for start in range(0, ids_here.shape[1], 128):
        ids = jnp.broadcast_to(ids_here[:, start : start + 128], (K, 128))
        left[:, start : start + 128] = test_matrix(seeds, ids, columns)
    project_half(left, held, other, None, copies)


def first_own_kernel(left, affinity, held, own, arrived):
    copies = load_half(affinity, held, arrived, lax.axis_index("core"))
    project_half(left, held, own, None, copies)


def solve_kernel(mine, theirs, held, left, other, *, scale):
    wide = held.shape[1]
    total = mine[...] + theirs[...]
    _, back = eliminate(total[:, wide:], total[:, :wide])
    left[...] = back.astype(jnp.bfloat16)
    project_half(left, held, other, scale)


def own_kernel(left, held, own, *, scale):
    project_half(left, held, own, scale)


def back_sums(half, held):
    both = jnp.zeros((2 * K, held.shape[1]), jnp.float32)
    gram = jnp.zeros((3 * K, 3 * K), jnp.float32)
    for step in range(4):
        parts = split_bf16(half[:, span(step)])
        both += jnp.dot(
            jnp.concatenate(parts[:2], axis=0),
            held[span(step), :],
            preferred_element_type=jnp.float32,
        )
        gram += triple_gram(parts)
    return both[:K] + both[K:], fold_gram(gram)


def back_own_kernel(half, held, packed):
    wide = held.shape[1]
    back, gram = back_sums(half, held)
    packed[:, :wide] = back
    packed[:, wide:] = jnp.zeros((K, 128), jnp.float32)
    packed[:, wide : wide + K] = gram


def back_other_kernel(half, held, before, packed):
    wide = held.shape[1]
    back, gram = back_sums(half, held)
    packed[:, :wide] = before[:, :wide] + back
    packed[:, wide:] = jnp.zeros((K, 128), jnp.float32)
    packed[:, wide : wide + K] = before[:, wide : wide + K] + gram


def gram_kernel(half, packed):
    gram = jnp.zeros((3 * K, 3 * K), jnp.float32)
    for step in range(4):
        gram += triple_gram(split_bf16(half[:, span(step)]))
    gram = fold_gram(gram)
    packed[...] = jnp.zeros_like(packed)
    packed[:, :K] = gram[:8]
    packed[:, K : 2 * K] = gram[8:]


def last_kernel(grams, half, basis, factor, *, scale):
    total = None
    for x in range(4):
        one, two, three, four = (grams[4 * x + k] for k in range(4))
        part = (one + three) + (two + four)
        total = part if total is None else total + part
    gram = jnp.concatenate([total[:, :K], total[:, K : 2 * K]], axis=0)
    place = pl.multiple_of(lax.axis_index("y") * PIECE, PIECE)
    lower, ortho = eliminate(gram, half[:, pl.ds(place, PIECE)])
    basis[...] = ortho * scale
    factor[...] = lower.T[:K, :] / scale


def call(kernel, outs, *args, spaces=None, scratch=(), flops=0):
    whole = pl.BlockSpec(memory_space=pltpu.VMEM)
    return pl.pallas_call(
        kernel,
        in_specs=spaces or [whole] * len(args),
        out_specs=[whole] * len(outs),
        out_shape=[jax.ShapeDtypeStruct(*out) for out in outs],
        scratch_shapes=scratch,
        cost_estimate=pl.CostEstimate(
            flops=flops, bytes_accessed=flops // K, transcendentals=0
        ),
        compiler_params=pltpu.CompilerParams(vmem_limit_bytes=32 * 1024 * 1024),
    )(*args)


def body(affinity, seed_values, sku_ids):
    local_rows, local_columns = affinity.shape
    total_columns = local_columns * 8
    total_rows = local_rows * 32
    f32 = jnp.float32
    half_out = ((K, local_rows // 2), f32)
    left_out = ((K, local_columns), jnp.bfloat16)
    packed_out = ((K, local_columns + 128), f32)
    pass_flops = K * local_rows * local_columns
    z = ("cube", "level")

    held_out = ((local_rows // 2, local_columns), jnp.bfloat16)
    far = pl.BlockSpec(memory_space=pltpu.HBM)
    near = pl.BlockSpec(memory_space=pltpu.VMEM)
    affinity, seed_values, sku_ids = (
        pltpu.with_memory_space_constraint(value, pltpu.HBM)
        for value in (affinity, seed_values, sku_ids.reshape(1, -1))
    )

    left, held_other, other = call(
        functools.partial(first_kernel, columns=total_columns),
        [left_out, held_out, half_out],
        seed_values,
        sku_ids,
        affinity,
        spaces=[far, far, far],
        scratch=[
            pltpu.SMEM(seed_values.shape, jnp.int32),
            pltpu.VMEM(sku_ids.shape, jnp.int32),
            pltpu.SemaphoreType.DMA((6,)),
        ],
        flops=pass_flops,
    )
    scale = 1.0 / math.sqrt(total_columns)
    for repeat in range(ITERS + 1):
        arriving = swap(other, "core", 2, 1)
        if repeat == 0:
            held_own, own = call(
                first_own_kernel,
                [held_out, half_out],
                left,
                affinity,
                spaces=[near, far],
                scratch=[pltpu.SemaphoreType.DMA((4,))],
                flops=pass_flops,
            )
        else:
            (own,) = call(
                functools.partial(own_kernel, scale=scale),
                [half_out],
                left,
                held_own,
                flops=pass_flops,
            )
        half = sum_four(own + arriving, "y", 4)
        if repeat < ITERS:
            sibling = swap(half, "core", 2, 1)
            (packed,) = call(back_own_kernel, [packed_out], half, held_own, flops=pass_flops)
            (packed,) = call(
                back_other_kernel, [packed_out], sibling, held_other, packed, flops=pass_flops
            )
            packed = sum_four(packed, "x", 4)
            packed = sum_four(packed, z, 8, (1, 6, 7))
            left, other = call(
                functools.partial(solve_kernel, scale=scale),
                [left_out, half_out],
                packed,
                swap(packed, z, 8, 2),
                held_other,
                flops=pass_flops,
            )
        else:
            (gram,) = call(gram_kernel, [((8, 128), f32)], half)
            gram = sum_four(gram, z + ("core",), 16, (1, 12, 13))
            spread = jnp.broadcast_to(gram[None], (16,) + gram.shape)
            grams = lax.all_to_all(spread, ("x", "level"), 0, 0)
            basis, factor = call(
                functools.partial(last_kernel, scale=math.sqrt(total_rows)),
                [((K, PIECE), f32), ((K, K), f32)],
                grams,
                half,
            )
    return basis, factor


def solution(mesh):
    names = ("x", "cube", "level", "y", "core")
    split = Mesh(mesh.devices.reshape(4, 2, 4, 4, 2), names)
    row, col = names[:3], names[3:]
    return jax.shard_map(
        body,
        mesh=split,
        in_specs=(P(row, col), P(), P(col)),
        out_specs=(P(None, row + col), P()),
        check_vma=False,
    )
```

```python
import functools
import math

import jax
import jax.numpy as jnp
from jax import lax
from jax.experimental import pallas as pl
from jax.experimental.pallas import tpu as pltpu
from jax.sharding import Mesh, PartitionSpec as P

ITERS = 2
K = 16
PIECE = 512


mix_first = -2048144789
mix_second = -1028477387
golden = -1640531535
salt_value = 1540483477


def shifted(value, amount):
    return lax.shift_right_logical(value, jnp.full(value.shape, amount, jnp.int32))


def scramble(value):
    value = jnp.bitwise_xor(value, shifted(value, 16))
    value = value * jnp.int32(mix_first)
    value = jnp.bitwise_xor(value, shifted(value, 13))
    value = value * jnp.int32(mix_second)
    return jnp.bitwise_xor(value, shifted(value, 16))


def test_matrix(seeds, sku_ids, total_columns):
    first = scramble(jnp.bitwise_xor(seeds, sku_ids * jnp.int32(golden)))
    second = scramble(jnp.bitwise_xor(first, jnp.int32(salt_value)))
    uniform_a = (shifted(first, 9) + 1).astype(jnp.float32) / 8388608.0
    uniform_b = (shifted(second, 9) + 1).astype(jnp.float32) / 8388608.0
    gauss = jnp.sqrt(-2.0 * jnp.log(uniform_a)) * jnp.cos(6.283185307179586 * uniform_b)
    return (gauss / math.sqrt(total_columns)).astype(jnp.bfloat16)


def swap(value, axis, count, offset):
    return lax.ppermute(value, axis, [(i, i ^ offset) for i in range(count)])


def sum_four(value, axis, count, offsets=(2, 1, 3)):
    one, two, three = (swap(value, axis, count, k) for k in offsets)
    return (value + two) + (one + three)


def span(step):
    return slice(step * PIECE, (step + 1) * PIECE)


def project_piece(left, rows, scale):
    part = lax.dot_general(
        left, rows, (((1,), (1,)), ((), ())), preferred_element_type=jnp.float32
    )
    return part if scale is None else part * scale


def split_bf16(value):
    high = value.astype(jnp.bfloat16)
    rest = value - high.astype(jnp.float32)
    low = rest.astype(jnp.bfloat16)
    last = (rest - low.astype(jnp.float32)).astype(jnp.bfloat16)
    return high, low, last


def triple_gram(parts):
    stacked = jnp.concatenate(parts, axis=0)
    return lax.dot_general(
        stacked, stacked, (((1,), (1,)), ((), ())), preferred_element_type=jnp.float32
    )


def fold_gram(gram):
    rows = (gram[2 * K :] + gram[K : 2 * K]) + gram[:K]
    return (rows[:, 2 * K :] + rows[:, K : 2 * K]) + rows[:, :K]


def eliminate(gram, right):
    row = lax.broadcasted_iota(jnp.int32, (K, 128), 0)
    lane = lax.broadcasted_iota(jnp.int32, (K, 128), 1)
    columns = [jnp.broadcast_to(gram[:, k : k + 1], (K, 128)) for k in range(K)]
    lower = jnp.zeros((K, 128), jnp.float32)
    pivots = jnp.ones((K, 128), jnp.float32)
    for k in range(K):
        column = columns[k]
        pivot = jnp.broadcast_to(column[k : k + 1, :], (K, 128))
        factor = column * (1.0 / pivot)
        lower = jnp.where((lane == k) & (row >= k), column / jnp.sqrt(pivot), lower)
        pivots = jnp.where(row == k, pivot, pivots)
        factor = jnp.where(row > k, factor, 0.0)
        for j in range(k + 1, K):
            columns[j] = columns[j] - factor * jnp.broadcast_to(column[j : j + 1, :], (K, 128))
        wide = jnp.tile(factor, (1, right.shape[1] // 128))
        right = right - wide * right[k : k + 1, :]
    root = jnp.sqrt(pivots)
    return lower, right / jnp.tile(root, (1, right.shape[1] // 128))


def load_half(affinity, held, arrived, side):
    copies = []
    for step in range(4):
        place = pl.multiple_of((2 * step + side) * PIECE, PIECE)
        copies.append(
            pltpu.make_async_copy(
                affinity.at[pl.ds(place, PIECE)], held.at[span(step)], arrived.at[step]
            )
        )
        copies[-1].start()
    return copies


def project_half(left, held, target, scale, copies=None):
    for step in range(4):
        if copies is not None:
            copies[step].wait()
        target[:, span(step)] = project_piece(left[...], held[span(step), :], scale)


def first_kernel(
    seed_values, sku_ids, affinity, left, held, other, seeds_here, ids_here, arrived, *, columns
):
    small = [
        pltpu.make_async_copy(seed_values, seeds_here, arrived.at[4]),
        pltpu.make_async_copy(sku_ids, ids_here, arrived.at[5]),
    ]
    for copy in small:
        copy.start()
    copies = load_half(affinity, held, arrived, 1 - lax.axis_index("core"))
    for copy in small:
        copy.wait()
    row = lax.broadcasted_iota(jnp.int32, (K, 128), 0)
    seeds = jnp.zeros((K, 128), jnp.int32)
    for k in range(K):
        seeds = jnp.where(row == k, seeds_here[k], seeds)
    for start in range(0, ids_here.shape[1], 128):
        ids = jnp.broadcast_to(ids_here[:, start : start + 128], (K, 128))
        left[:, start : start + 128] = test_matrix(seeds, ids, columns)
    project_half(left, held, other, None, copies)


def first_own_kernel(left, affinity, held, own, arrived):
    copies = load_half(affinity, held, arrived, lax.axis_index("core"))
    project_half(left, held, own, None, copies)


def solve_kernel(mine, theirs, held, left, other, *, scale):
    wide = held.shape[1]
    total = mine[...] + theirs[...]
    _, back = eliminate(total[:, wide:], total[:, :wide])
    left[...] = back.astype(jnp.bfloat16)
    project_half(left, held, other, scale)


def own_kernel(left, held, own, *, scale):
    project_half(left, held, own, scale)


def back_sums(half, held):
    both = jnp.zeros((2 * K, held.shape[1]), jnp.float32)
    gram = jnp.zeros((3 * K, 3 * K), jnp.float32)
    for step in range(4):
        parts = split_bf16(half[:, span(step)])
        both += jnp.dot(
            jnp.concatenate(parts[:2], axis=0),
            held[span(step), :],
            preferred_element_type=jnp.float32,
        )
        gram += triple_gram(parts)
    return both[:K] + both[K:], fold_gram(gram)


def back_own_kernel(half, held, packed):
    wide = held.shape[1]
    back, gram = back_sums(half, held)
    packed[:, :wide] = back
    packed[:, wide:] = jnp.zeros((K, 128), jnp.float32)
    packed[:, wide : wide + K] = gram


def back_other_kernel(half, held, before, packed):
    wide = held.shape[1]
    back, gram = back_sums(half, held)
    packed[:, :wide] = before[:, :wide] + back
    packed[:, wide:] = jnp.zeros((K, 128), jnp.float32)
    packed[:, wide : wide + K] = before[:, wide : wide + K] + gram


def gram_kernel(half, packed):
    gram = jnp.zeros((3 * K, 3 * K), jnp.float32)
    for step in range(4):
        gram += triple_gram(split_bf16(half[:, span(step)]))
    gram = fold_gram(gram)
    packed[...] = jnp.zeros_like(packed)
    packed[:, :K] = gram[:8]
    packed[:, K : 2 * K] = gram[8:]


def last_kernel(grams, half, basis, factor, *, scale):
    total = None
    for x in range(4):
        one, two, three, four = (grams[4 * x + k] for k in range(4))
        part = (one + three) + (two + four)
        total = part if total is None else total + part
    gram = jnp.concatenate([total[:, :K], total[:, K : 2 * K]], axis=0)
    place = pl.multiple_of(lax.axis_index("y") * PIECE, PIECE)
    lower, ortho = eliminate(gram, half[:, pl.ds(place, PIECE)])
    basis[...] = ortho * scale
    factor[...] = lower.T[:K, :] / scale


def call(kernel, outs, *args, spaces=None, scratch=(), flops=0):
    whole = pl.BlockSpec(memory_space=pltpu.VMEM)
    return pl.pallas_call(
        kernel,
        in_specs=spaces or [whole] * len(args),
        out_specs=[whole] * len(outs),
        out_shape=[jax.ShapeDtypeStruct(*out) for out in outs],
        scratch_shapes=scratch,
        cost_estimate=pl.CostEstimate(
            flops=flops, bytes_accessed=flops // K, transcendentals=0
        ),
        compiler_params=pltpu.CompilerParams(vmem_limit_bytes=32 * 1024 * 1024),
    )(*args)


def body(affinity, seed_values, sku_ids):
    local_rows, local_columns = affinity.shape
    total_columns = local_columns * 8
    total_rows = local_rows * 32
    f32 = jnp.float32
    half_out = ((K, local_rows // 2), f32)
    left_out = ((K, local_columns), jnp.bfloat16)
    packed_out = ((K, local_columns + 128), f32)
    pass_flops = K * local_rows * local_columns
    z = ("cube", "level")

    held_out = ((local_rows // 2, local_columns), jnp.bfloat16)
    far = pl.BlockSpec(memory_space=pltpu.HBM)
    near = pl.BlockSpec(memory_space=pltpu.VMEM)
    affinity, seed_values, sku_ids = (
        pltpu.with_memory_space_constraint(value, pltpu.HBM)
        for value in (affinity, seed_values, sku_ids.reshape(1, -1))
    )

    left, held_other, other = call(
        functools.partial(first_kernel, columns=total_columns),
        [left_out, held_out, half_out],
        seed_values,
        sku_ids,
        affinity,
        spaces=[far, far, far],
        scratch=[
            pltpu.SMEM(seed_values.shape, jnp.int32),
            pltpu.VMEM(sku_ids.shape, jnp.int32),
            pltpu.SemaphoreType.DMA((6,)),
        ],
        flops=pass_flops,
    )
    scale = 1.0 / math.sqrt(total_columns)
    for repeat in range(ITERS + 1):
        arriving = swap(other, "core", 2, 1)
        if repeat == 0:
            held_own, own = call(
                first_own_kernel,
                [held_out, half_out],
                left,
                affinity,
                spaces=[near, far],
                scratch=[pltpu.SemaphoreType.DMA((4,))],
                flops=pass_flops,
            )
        else:
            (own,) = call(
                functools.partial(own_kernel, scale=scale),
                [half_out],
                left,
                held_own,
                flops=pass_flops,
            )
        half = sum_four(own + arriving, "y", 4)
        if repeat < ITERS:
            sibling = swap(half, "core", 2, 1)
            (packed,) = call(back_own_kernel, [packed_out], half, held_own, flops=pass_flops)
            (packed,) = call(
                back_other_kernel, [packed_out], sibling, held_other, packed, flops=pass_flops
            )
            packed = sum_four(packed, "x", 4)
            packed = sum_four(packed, z, 8)
            left, other = call(
                functools.partial(solve_kernel, scale=scale),
                [left_out, half_out],
                packed,
                swap(packed, z, 8, 6),
                held_other,
                flops=pass_flops,
            )
        else:
            (gram,) = call(gram_kernel, [((8, 128), f32)], half)
            gram = sum_four(gram, z + ("core",), 16, (12, 1, 13))
            spread = jnp.broadcast_to(gram[None], (16,) + gram.shape)
            grams = lax.all_to_all(spread, ("x", "level"), 0, 0)
            basis, factor = call(
                functools.partial(last_kernel, scale=math.sqrt(total_rows)),
                [((K, PIECE), f32), ((K, K), f32)],
                grams,
                half,
            )
    return basis, factor


def solution(mesh):
    names = ("x", "cube", "level", "y", "core")
    split = Mesh(mesh.devices.reshape(4, 2, 4, 4, 2), names)
    row, col = names[:3], names[3:]
    return jax.shard_map(
        body,
        mesh=split,
        in_specs=(P(row, col), P(), P(col)),
        out_specs=(P(None, row + col), P()),
        check_vma=False,
    )
```

```python
import functools
import math

import jax
import jax.numpy as jnp
from jax import lax
from jax.experimental import pallas as pl
from jax.experimental.pallas import tpu as pltpu
from jax.sharding import Mesh, PartitionSpec as P

ITERS = 2
K = 16
PIECE = 512


mix_first = -2048144789
mix_second = -1028477387
golden = -1640531535
salt_value = 1540483477


def shifted(value, amount):
    return lax.shift_right_logical(value, jnp.full(value.shape, amount, jnp.int32))


def scramble(value):
    value = jnp.bitwise_xor(value, shifted(value, 16))
    value = value * jnp.int32(mix_first)
    value = jnp.bitwise_xor(value, shifted(value, 13))
    value = value * jnp.int32(mix_second)
    return jnp.bitwise_xor(value, shifted(value, 16))


def test_matrix(seeds, sku_ids, total_columns):
    first = scramble(jnp.bitwise_xor(seeds, sku_ids * jnp.int32(golden)))
    second = scramble(jnp.bitwise_xor(first, jnp.int32(salt_value)))
    uniform_a = (shifted(first, 9) + 1).astype(jnp.float32) / 8388608.0
    uniform_b = (shifted(second, 9) + 1).astype(jnp.float32) / 8388608.0
    gauss = jnp.sqrt(-2.0 * jnp.log(uniform_a)) * jnp.cos(6.283185307179586 * uniform_b)
    return (gauss / math.sqrt(total_columns)).astype(jnp.bfloat16)


def swap(value, axis, count, offset):
    return lax.ppermute(value, axis, [(i, i ^ offset) for i in range(count)])


def sum_four(value, axis, count, offsets=(2, 1, 3)):
    one, two, three = (swap(value, axis, count, k) for k in offsets)
    return (value + two) + (one + three)


def span(step):
    return slice(step * PIECE, (step + 1) * PIECE)


def project_piece(left, rows, scale):
    part = lax.dot_general(
        left, rows, (((1,), (1,)), ((), ())), preferred_element_type=jnp.float32
    )
    return part if scale is None else part * scale


def split_bf16(value):
    high = value.astype(jnp.bfloat16)
    rest = value - high.astype(jnp.float32)
    low = rest.astype(jnp.bfloat16)
    last = (rest - low.astype(jnp.float32)).astype(jnp.bfloat16)
    return high, low, last


def triple_gram(parts):
    stacked = jnp.concatenate(parts, axis=0)
    return lax.dot_general(
        stacked, stacked, (((1,), (1,)), ((), ())), preferred_element_type=jnp.float32
    )


def fold_gram(gram):
    rows = (gram[2 * K :] + gram[K : 2 * K]) + gram[:K]
    return (rows[:, 2 * K :] + rows[:, K : 2 * K]) + rows[:, :K]


def eliminate(gram, right):
    row = lax.broadcasted_iota(jnp.int32, (K, 128), 0)
    lane = lax.broadcasted_iota(jnp.int32, (K, 128), 1)
    columns = [jnp.broadcast_to(gram[:, k : k + 1], (K, 128)) for k in range(K)]
    lower = jnp.zeros((K, 128), jnp.float32)
    pivots = jnp.ones((K, 128), jnp.float32)
    for k in range(K):
        column = columns[k]
        pivot = jnp.broadcast_to(column[k : k + 1, :], (K, 128))
        factor = column * (1.0 / pivot)
        lower = jnp.where((lane == k) & (row >= k), column / jnp.sqrt(pivot), lower)
        pivots = jnp.where(row == k, pivot, pivots)
        factor = jnp.where(row > k, factor, 0.0)
        for j in range(k + 1, K):
            columns[j] = columns[j] - factor * jnp.broadcast_to(column[j : j + 1, :], (K, 128))
        wide = jnp.tile(factor, (1, right.shape[1] // 128))
        right = right - wide * right[k : k + 1, :]
    root = jnp.sqrt(pivots)
    return lower, right / jnp.tile(root, (1, right.shape[1] // 128))


def load_half(affinity, held, arrived, side):
    copies = []
    for step in range(4):
        place = pl.multiple_of((2 * step + side) * PIECE, PIECE)
        copies.append(
            pltpu.make_async_copy(
                affinity.at[pl.ds(place, PIECE)], held.at[span(step)], arrived.at[step]
            )
        )
        copies[-1].start()
    return copies


def project_half(left, held, target, scale, copies=None):
    for step in range(4):
        if copies is not None:
            copies[step].wait()
        target[:, span(step)] = project_piece(left[...], held[span(step), :], scale)


def first_kernel(
    seed_values,
    sku_ids,
    affinity,
    left,
    held_other,
    held_own,
    other,
    seeds_here,
    ids_here,
    small_arrived,
    other_arrived,
    own_arrived,
    *,
    columns,
):
    core = lax.axis_index("core")
    small = [
        pltpu.make_async_copy(seed_values, seeds_here, small_arrived.at[0]),
        pltpu.make_async_copy(sku_ids, ids_here, small_arrived.at[1]),
    ]
    for copy in small:
        copy.start()
    copies = load_half(affinity, held_other, other_arrived, 1 - core)
    later = load_half(affinity, held_own, own_arrived, core)
    for copy in small:
        copy.wait()
    row = lax.broadcasted_iota(jnp.int32, (K, 128), 0)
    seeds = jnp.zeros((K, 128), jnp.int32)
    for k in range(K):
        seeds = jnp.where(row == k, seeds_here[k], seeds)
    for start in range(0, ids_here.shape[1], 128):
        ids = jnp.broadcast_to(ids_here[:, start : start + 128], (K, 128))
        left[:, start : start + 128] = test_matrix(seeds, ids, columns)
    project_half(left, held_other, other, None, copies)
    for copy in later:
        copy.wait()


def solve_kernel(mine, theirs, held, left, other, *, scale):
    total = mine[...] + theirs[...]
    tiles = held.shape[1] // 128
    back = jnp.concatenate([total[tile * K : (tile + 1) * K] for tile in range(tiles)], axis=1)
    _, back = eliminate(unpack_gram(total[tiles * K :]), back)
    left[...] = back.astype(jnp.bfloat16)
    project_half(left, held, other, scale)


def own_kernel(left, held, own, *, scale):
    project_half(left, held, own, scale)


def back_sums(half, held):
    both = jnp.zeros((2 * K, held.shape[1]), jnp.float32)
    gram = jnp.zeros((3 * K, 3 * K), jnp.float32)
    for step in range(4):
        parts = split_bf16(half[:, span(step)])
        both += jnp.dot(
            jnp.concatenate(parts[:2], axis=0),
            held[span(step), :],
            preferred_element_type=jnp.float32,
        )
        gram += triple_gram(parts)
    return both[:K] + both[K:], fold_gram(gram)


def pack_gram(gram):
    blank = jnp.zeros((8, 128 - 2 * K), jnp.float32)
    return jnp.concatenate([gram[:8], gram[8:], blank], axis=1)


def unpack_gram(packed):
    return jnp.concatenate([packed[:, :K], packed[:, K : 2 * K]], axis=0)


def back_own_kernel(half, held, packed):
    back, gram = back_sums(half, held)
    tiles = held.shape[1] // 128
    for tile in range(tiles):
        packed[tile * K : (tile + 1) * K, :] = back[:, tile * 128 : (tile + 1) * 128]
    packed[tiles * K :, :] = pack_gram(gram)


def back_other_kernel(half, held, before, packed):
    back_own_kernel(half, held, packed)
    packed[...] = before[...] + packed[...]


def gram_kernel(half, packed):
    gram = jnp.zeros((3 * K, 3 * K), jnp.float32)
    for step in range(4):
        gram += triple_gram(split_bf16(half[:, span(step)]))
    packed[...] = pack_gram(fold_gram(gram))


def last_kernel(grams, half, basis, factor, *, scale):
    total = None
    for x in range(4):
        one, two, three, four = (grams[4 * x + k] for k in range(4))
        part = (one + three) + (two + four)
        total = part if total is None else total + part
    gram = unpack_gram(total)
    place = pl.multiple_of(lax.axis_index("y") * PIECE, PIECE)
    lower, ortho = eliminate(gram, half[:, pl.ds(place, PIECE)])
    basis[...] = ortho * scale
    factor[...] = lower.T[:K, :] / scale


def call(kernel, outs, *args, spaces=None, scratch=(), flops=0):
    whole = pl.BlockSpec(memory_space=pltpu.VMEM)
    return pl.pallas_call(
        kernel,
        in_specs=spaces or [whole] * len(args),
        out_specs=[whole] * len(outs),
        out_shape=[jax.ShapeDtypeStruct(*out) for out in outs],
        scratch_shapes=scratch,
        cost_estimate=pl.CostEstimate(
            flops=flops, bytes_accessed=flops // K, transcendentals=0
        ),
        compiler_params=pltpu.CompilerParams(vmem_limit_bytes=32 * 1024 * 1024),
    )(*args)


def body(affinity, seed_values, sku_ids):
    local_rows, local_columns = affinity.shape
    total_columns = local_columns * 8
    total_rows = local_rows * 32
    f32 = jnp.float32
    half_out = ((K, local_rows // 2), f32)
    left_out = ((K, local_columns), jnp.bfloat16)
    packed_out = ((local_columns // 128 * K + 8, 128), f32)
    pass_flops = K * local_rows * local_columns
    z = ("cube", "level")

    held_out = ((local_rows // 2, local_columns), jnp.bfloat16)
    far = pl.BlockSpec(memory_space=pltpu.HBM)
    affinity, seed_values, sku_ids = (
        pltpu.with_memory_space_constraint(value, pltpu.HBM)
        for value in (affinity, seed_values, sku_ids.reshape(1, -1))
    )

    left, held_other, held_own, other = call(
        functools.partial(first_kernel, columns=total_columns),
        [left_out, held_out, held_out, half_out],
        seed_values,
        sku_ids,
        affinity,
        spaces=[far, far, far],
        scratch=[
            pltpu.SMEM(seed_values.shape, jnp.int32),
            pltpu.VMEM(sku_ids.shape, jnp.int32),
            pltpu.SemaphoreType.DMA((2,)),
            pltpu.SemaphoreType.DMA((4,)),
            pltpu.SemaphoreType.DMA((4,)),
        ],
        flops=pass_flops,
    )
    scale = 1.0 / math.sqrt(total_columns)
    for repeat in range(ITERS + 1):
        arriving = swap(other, "core", 2, 1)
        own_scale = None if repeat == 0 else scale
        (own,) = call(
            functools.partial(own_kernel, scale=own_scale),
            [half_out],
            left,
            held_own,
            flops=pass_flops,
        )
        half = sum_four(own + arriving, "y", 4)
        if repeat < ITERS:
            sibling = swap(half, "core", 2, 1)
            (packed,) = call(back_own_kernel, [packed_out], half, held_own, flops=pass_flops)
            (packed,) = call(
                back_other_kernel, [packed_out], sibling, held_other, packed, flops=pass_flops
            )
            packed = sum_four(packed, "x", 4)
            packed = sum_four(packed, z, 8)
            left, other = call(
                functools.partial(solve_kernel, scale=scale),
                [left_out, half_out],
                packed,
                swap(packed, z, 8, 6),
                held_other,
                flops=pass_flops,
            )
        else:
            (gram,) = call(gram_kernel, [((8, 128), f32)], half)
            gram = sum_four(gram, z + ("core",), 16, (12, 1, 13))
            spread = jnp.broadcast_to(gram[None], (16,) + gram.shape)
            grams = lax.all_to_all(spread, ("x", "level"), 0, 0)
            basis, factor = call(
                functools.partial(last_kernel, scale=math.sqrt(total_rows)),
                [((K, PIECE), f32), ((K, K), f32)],
                grams,
                half,
            )
    return basis, factor


def solution(mesh):
    names = ("x", "cube", "level", "y", "core")
    split = Mesh(mesh.devices.reshape(4, 2, 4, 4, 2), names)
    row, col = names[:3], names[3:]
    return jax.shard_map(
        body,
        mesh=split,
        in_specs=(P(row, col), P(), P(col)),
        out_specs=(P(None, row + col), P()),
        check_vma=False,
    )
```

```python
import functools
import math

import jax
import jax.numpy as jnp
from jax import lax
from jax.experimental import pallas as pl
from jax.experimental.pallas import tpu as pltpu
from jax.sharding import Mesh, PartitionSpec as P

ITERS = 2
K = 16
PIECE = 512


mix_first = -2048144789
mix_second = -1028477387
golden = -1640531535
salt_value = 1540483477


def shifted(value, amount):
    return lax.shift_right_logical(value, jnp.full(value.shape, amount, jnp.int32))


def scramble(value):
    value = jnp.bitwise_xor(value, shifted(value, 16))
    value = value * jnp.int32(mix_first)
    value = jnp.bitwise_xor(value, shifted(value, 13))
    value = value * jnp.int32(mix_second)
    return jnp.bitwise_xor(value, shifted(value, 16))


def test_matrix(seeds, sku_ids, total_columns):
    first = scramble(jnp.bitwise_xor(seeds, sku_ids * jnp.int32(golden)))
    second = scramble(jnp.bitwise_xor(first, jnp.int32(salt_value)))
    uniform_a = (shifted(first, 9) + 1).astype(jnp.float32) / 8388608.0
    uniform_b = (shifted(second, 9) + 1).astype(jnp.float32) / 8388608.0
    gauss = jnp.sqrt(-2.0 * jnp.log(uniform_a)) * jnp.cos(6.283185307179586 * uniform_b)
    return (gauss / math.sqrt(total_columns)).astype(jnp.bfloat16)


def swap(value, axis, count, offset):
    return lax.ppermute(value, axis, [(i, i ^ offset) for i in range(count)])


def sum_four(value, axis, count, offsets=(2, 1, 3)):
    one, two, three = (swap(value, axis, count, k) for k in offsets)
    return (value + two) + (one + three)


def span(step):
    return slice(step * PIECE, (step + 1) * PIECE)


def project_piece(left, rows, scale):
    part = lax.dot_general(
        left, rows, (((1,), (1,)), ((), ())), preferred_element_type=jnp.float32
    )
    return part if scale is None else part * scale


def split_bf16(value):
    high = value.astype(jnp.bfloat16)
    rest = value - high.astype(jnp.float32)
    low = rest.astype(jnp.bfloat16)
    last = (rest - low.astype(jnp.float32)).astype(jnp.bfloat16)
    return high, low, last


def triple_gram(parts):
    stacked = jnp.concatenate(parts, axis=0)
    return lax.dot_general(
        stacked, stacked, (((1,), (1,)), ((), ())), preferred_element_type=jnp.float32
    )


def fold_gram(gram):
    rows = (gram[2 * K :] + gram[K : 2 * K]) + gram[:K]
    return (rows[:, 2 * K :] + rows[:, K : 2 * K]) + rows[:, :K]


def eliminate(gram, right):
    row = lax.broadcasted_iota(jnp.int32, (K, 128), 0)
    lane = lax.broadcasted_iota(jnp.int32, (K, 128), 1)
    columns = [jnp.broadcast_to(gram[:, k : k + 1], (K, 128)) for k in range(K)]
    lower = jnp.zeros((K, 128), jnp.float32)
    pivots = jnp.ones((K, 128), jnp.float32)
    for k in range(K):
        column = columns[k]
        pivot = jnp.broadcast_to(column[k : k + 1, :], (K, 128))
        factor = column * (1.0 / pivot)
        lower = jnp.where((lane == k) & (row >= k), column / jnp.sqrt(pivot), lower)
        pivots = jnp.where(row == k, pivot, pivots)
        factor = jnp.where(row > k, factor, 0.0)
        for j in range(k + 1, K):
            columns[j] = columns[j] - factor * jnp.broadcast_to(column[j : j + 1, :], (K, 128))
        wide = jnp.tile(factor, (1, right.shape[1] // 128))
        right = right - wide * right[k : k + 1, :]
    root = jnp.sqrt(pivots)
    return lower, right / jnp.tile(root, (1, right.shape[1] // 128))


def load_half(affinity, held, arrived, side):
    copies = []
    for step in range(4):
        place = pl.multiple_of((2 * step + side) * PIECE, PIECE)
        copies.append(
            pltpu.make_async_copy(
                affinity.at[pl.ds(place, PIECE)], held.at[span(step)], arrived.at[step]
            )
        )
        copies[-1].start()
    return copies


def project_half(left, held, target, scale, copies=None):
    for step in range(4):
        if copies is not None:
            copies[step].wait()
        target[:, span(step)] = project_piece(left[...], held[span(step), :], scale)


def first_kernel(
    seed_values,
    sku_ids,
    affinity,
    left,
    held_other,
    held_own,
    other,
    seeds_here,
    ids_here,
    small_arrived,
    other_arrived,
    own_arrived,
    *,
    columns,
):
    core = lax.axis_index("core")
    small = [
        pltpu.make_async_copy(seed_values, seeds_here, small_arrived.at[0]),
        pltpu.make_async_copy(sku_ids, ids_here, small_arrived.at[1]),
    ]
    copies = load_half(affinity, held_other, other_arrived, 1 - core)
    for copy in small:
        copy.start()
    later = load_half(affinity, held_own, own_arrived, core)
    for copy in small:
        copy.wait()
    row = lax.broadcasted_iota(jnp.int32, (K, 128), 0)
    seeds = jnp.zeros((K, 128), jnp.int32)
    for k in range(K):
        seeds = jnp.where(row == k, seeds_here[k], seeds)
    for start in range(0, ids_here.shape[1], 128):
        ids = jnp.broadcast_to(ids_here[:, start : start + 128], (K, 128))
        left[:, start : start + 128] = test_matrix(seeds, ids, columns)
    project_half(left, held_other, other, None, copies)
    for copy in later:
        copy.wait()


def solve_kernel(mine, theirs, held, left, other, *, scale):
    total = mine[...] + theirs[...]
    tiles = held.shape[1] // 128
    back = jnp.concatenate([total[tile * K : (tile + 1) * K] for tile in range(tiles)], axis=1)
    _, back = eliminate(unpack_gram(total[tiles * K :]), back)
    left[...] = back.astype(jnp.bfloat16)
    project_half(left, held, other, scale)


def own_kernel(left, held, own, *, scale):
    project_half(left, held, own, scale)


def back_sums(half, held):
    both = jnp.zeros((2 * K, held.shape[1]), jnp.float32)
    gram = jnp.zeros((3 * K, 3 * K), jnp.float32)
    for step in range(4):
        parts = split_bf16(half[:, span(step)])
        both += jnp.dot(
            jnp.concatenate(parts[:2], axis=0),
            held[span(step), :],
            preferred_element_type=jnp.float32,
        )
        gram += triple_gram(parts)
    return both[:K] + both[K:], fold_gram(gram)


def pack_gram(gram):
    blank = jnp.zeros((8, 128 - 2 * K), jnp.float32)
    return jnp.concatenate([gram[:8], gram[8:], blank], axis=1)


def unpack_gram(packed):
    return jnp.concatenate([packed[:, :K], packed[:, K : 2 * K]], axis=0)


def back_own_kernel(half, held, packed):
    back, gram = back_sums(half, held)
    tiles = held.shape[1] // 128
    for tile in range(tiles):
        packed[tile * K : (tile + 1) * K, :] = back[:, tile * 128 : (tile + 1) * 128]
    packed[tiles * K :, :] = pack_gram(gram)


def back_other_kernel(half, held, before, packed):
    back_own_kernel(half, held, packed)
    packed[...] = before[...] + packed[...]


def gram_kernel(half, packed):
    gram = jnp.zeros((3 * K, 3 * K), jnp.float32)
    for step in range(4):
        gram += triple_gram(split_bf16(half[:, span(step)]))
    packed[...] = pack_gram(fold_gram(gram))


def last_kernel(grams, half, basis, factor, *, scale):
    total = None
    for x in range(4):
        one, two, three, four = (grams[4 * x + k] for k in range(4))
        part = (one + three) + (two + four)
        total = part if total is None else total + part
    gram = unpack_gram(total)
    place = pl.multiple_of(lax.axis_index("y") * PIECE, PIECE)
    lower, ortho = eliminate(gram, half[:, pl.ds(place, PIECE)])
    basis[...] = ortho * scale
    factor[...] = lower.T[:K, :] / scale


def call(kernel, outs, *args, spaces=None, scratch=(), flops=0):
    whole = pl.BlockSpec(memory_space=pltpu.VMEM)
    return pl.pallas_call(
        kernel,
        in_specs=spaces or [whole] * len(args),
        out_specs=[whole] * len(outs),
        out_shape=[jax.ShapeDtypeStruct(*out) for out in outs],
        scratch_shapes=scratch,
        cost_estimate=pl.CostEstimate(
            flops=flops, bytes_accessed=flops // K, transcendentals=0
        ),
        compiler_params=pltpu.CompilerParams(vmem_limit_bytes=32 * 1024 * 1024),
    )(*args)


def body(affinity, seed_values, sku_ids):
    local_rows, local_columns = affinity.shape
    total_columns = local_columns * 8
    total_rows = local_rows * 32
    f32 = jnp.float32
    half_out = ((K, local_rows // 2), f32)
    left_out = ((K, local_columns), jnp.bfloat16)
    packed_out = ((local_columns // 128 * K + 8, 128), f32)
    pass_flops = K * local_rows * local_columns
    z = ("cube", "level")

    held_out = ((local_rows // 2, local_columns), jnp.bfloat16)
    far = pl.BlockSpec(memory_space=pltpu.HBM)
    affinity, seed_values, sku_ids = (
        pltpu.with_memory_space_constraint(value, pltpu.HBM)
        for value in (affinity, seed_values, sku_ids.reshape(1, -1))
    )

    left, held_other, held_own, other = call(
        functools.partial(first_kernel, columns=total_columns),
        [left_out, held_out, held_out, half_out],
        seed_values,
        sku_ids,
        affinity,
        spaces=[far, far, far],
        scratch=[
            pltpu.SMEM(seed_values.shape, jnp.int32),
            pltpu.VMEM(sku_ids.shape, jnp.int32),
            pltpu.SemaphoreType.DMA((2,)),
            pltpu.SemaphoreType.DMA((4,)),
            pltpu.SemaphoreType.DMA((4,)),
        ],
        flops=pass_flops,
    )
    scale = 1.0 / math.sqrt(total_columns)
    for repeat in range(ITERS + 1):
        arriving = swap(other, "core", 2, 1)
        own_scale = None if repeat == 0 else scale
        (own,) = call(
            functools.partial(own_kernel, scale=own_scale),
            [half_out],
            left,
            held_own,
            flops=pass_flops,
        )
        half = sum_four(own + arriving, "y", 4)
        if repeat < ITERS:
            sibling = swap(half, "core", 2, 1)
            (packed,) = call(back_own_kernel, [packed_out], half, held_own, flops=pass_flops)
            (packed,) = call(
                back_other_kernel, [packed_out], sibling, held_other, packed, flops=pass_flops
            )
            packed = sum_four(packed, "x", 4, (3, 1, 2))
            packed = sum_four(packed, z, 8)
            left, other = call(
                functools.partial(solve_kernel, scale=scale),
                [left_out, half_out],
                packed,
                swap(packed, z, 8, 6),
                held_other,
                flops=pass_flops,
            )
        else:
            (gram,) = call(gram_kernel, [((8, 128), f32)], half)
            gram = sum_four(gram, z + ("core",), 16, (12, 1, 13))
            spread = jnp.broadcast_to(gram[None], (16,) + gram.shape)
            grams = lax.all_to_all(spread, ("x", "level"), 0, 0)
            basis, factor = call(
                functools.partial(last_kernel, scale=math.sqrt(total_rows)),
                [((K, PIECE), f32), ((K, K), f32)],
                grams,
                half,
            )
    return basis, factor


def solution(mesh):
    names = ("x", "cube", "level", "y", "core")
    split = Mesh(mesh.devices.reshape(4, 2, 4, 4, 2), names)
    row, col = names[:3], names[3:]
    return jax.shard_map(
        body,
        mesh=split,
        in_specs=(P(row, col), P(), P(col)),
        out_specs=(P(None, row + col), P()),
        check_vma=False,
    )
```

```python
import functools
import math

import jax
import jax.numpy as jnp
from jax import lax
from jax.experimental import pallas as pl
from jax.experimental.pallas import tpu as pltpu
from jax.sharding import Mesh, PartitionSpec as P

ITERS = 2
K = 16
PIECE = 512


mix_first = -2048144789
mix_second = -1028477387
golden = -1640531535
salt_value = 1540483477


def shifted(value, amount):
    return lax.shift_right_logical(value, jnp.full(value.shape, amount, jnp.int32))


def scramble(value):
    value = jnp.bitwise_xor(value, shifted(value, 16))
    value = value * jnp.int32(mix_first)
    value = jnp.bitwise_xor(value, shifted(value, 13))
    value = value * jnp.int32(mix_second)
    return jnp.bitwise_xor(value, shifted(value, 16))


def test_matrix(seeds, sku_ids, total_columns):
    first = scramble(jnp.bitwise_xor(seeds, sku_ids * jnp.int32(golden)))
    second = scramble(jnp.bitwise_xor(first, jnp.int32(salt_value)))
    uniform_a = (shifted(first, 9) + 1).astype(jnp.float32) / 8388608.0
    uniform_b = (shifted(second, 9) + 1).astype(jnp.float32) / 8388608.0
    gauss = jnp.sqrt(-2.0 * jnp.log(uniform_a)) * jnp.cos(6.283185307179586 * uniform_b)
    return (gauss / math.sqrt(total_columns)).astype(jnp.bfloat16)


def swap(value, axis, count, offset):
    return lax.ppermute(value, axis, [(i, i ^ offset) for i in range(count)])


def sum_four(value, axis, count, offsets=(2, 1, 3)):
    one, two, three = (swap(value, axis, count, k) for k in offsets)
    return (value + two) + (one + three)


def span(step):
    return slice(step * PIECE, (step + 1) * PIECE)


def project_piece(left, rows, scale):
    part = lax.dot_general(
        left, rows, (((1,), (1,)), ((), ())), preferred_element_type=jnp.float32
    )
    return part if scale is None else part * scale


def split_bf16(value):
    high = value.astype(jnp.bfloat16)
    rest = value - high.astype(jnp.float32)
    low = rest.astype(jnp.bfloat16)
    last = (rest - low.astype(jnp.float32)).astype(jnp.bfloat16)
    return high, low, last


def triple_gram(parts):
    stacked = jnp.concatenate(parts, axis=0)
    return lax.dot_general(
        stacked, stacked, (((1,), (1,)), ((), ())), preferred_element_type=jnp.float32
    )


def fold_gram(gram):
    rows = (gram[2 * K :] + gram[K : 2 * K]) + gram[:K]
    return (rows[:, 2 * K :] + rows[:, K : 2 * K]) + rows[:, :K]


def eliminate(gram, right):
    row = lax.broadcasted_iota(jnp.int32, (K, 128), 0)
    lane = lax.broadcasted_iota(jnp.int32, (K, 128), 1)
    columns = [jnp.broadcast_to(gram[:, k : k + 1], (K, 128)) for k in range(K)]
    lower = jnp.zeros((K, 128), jnp.float32)
    pivots = jnp.ones((K, 128), jnp.float32)
    for k in range(K):
        column = columns[k]
        pivot = jnp.broadcast_to(column[k : k + 1, :], (K, 128))
        factor = column * (1.0 / pivot)
        lower = jnp.where((lane == k) & (row >= k), column / jnp.sqrt(pivot), lower)
        pivots = jnp.where(row == k, pivot, pivots)
        factor = jnp.where(row > k, factor, 0.0)
        for j in range(k + 1, K):
            columns[j] = columns[j] - factor * jnp.broadcast_to(column[j : j + 1, :], (K, 128))
        wide = jnp.tile(factor, (1, right.shape[1] // 128))
        right = right - wide * right[k : k + 1, :]
    root = jnp.sqrt(pivots)
    return lower, right / jnp.tile(root, (1, right.shape[1] // 128))


def load_half(affinity, held, arrived, side):
    copies = []
    for step in range(4):
        place = pl.multiple_of((2 * step + side) * PIECE, PIECE)
        copies.append(
            pltpu.make_async_copy(
                affinity.at[pl.ds(place, PIECE)], held.at[span(step)], arrived.at[step]
            )
        )
        copies[-1].start()
    return copies


def project_half(left, held, target, scale, copies=None):
    for step in range(4):
        if copies is not None:
            copies[step].wait()
        target[:, span(step)] = project_piece(left[...], held[span(step), :], scale)


def first_kernel(
    seed_values,
    sku_ids,
    affinity,
    left,
    held_other,
    held_own,
    other,
    seeds_here,
    ids_here,
    small_arrived,
    other_arrived,
    own_arrived,
    *,
    columns,
):
    core = lax.axis_index("core")
    small = [
        pltpu.make_async_copy(seed_values, seeds_here, small_arrived.at[0]),
        pltpu.make_async_copy(sku_ids, ids_here, small_arrived.at[1]),
    ]
    for copy in small:
        copy.start()
    copies = load_half(affinity, held_other, other_arrived, 1 - core)
    for copy in small:
        copy.wait()
    row = lax.broadcasted_iota(jnp.int32, (K, 128), 0)
    seeds = jnp.zeros((K, 128), jnp.int32)
    for k in range(K):
        seeds = jnp.where(row == k, seeds_here[k], seeds)
    for start in range(0, ids_here.shape[1], 128):
        ids = jnp.broadcast_to(ids_here[:, start : start + 128], (K, 128))
        left[:, start : start + 128] = test_matrix(seeds, ids, columns)
    later = load_half(affinity, held_own, own_arrived, core)
    project_half(left, held_other, other, None, copies)
    for copy in later:
        copy.wait()


def solve_kernel(mine, theirs, held, left, other, *, scale):
    total = mine[...] + theirs[...]
    tiles = held.shape[1] // 128
    back = jnp.concatenate([total[tile * K : (tile + 1) * K] for tile in range(tiles)], axis=1)
    _, back = eliminate(unpack_gram(total[tiles * K :]), back)
    left[...] = back.astype(jnp.bfloat16)
    project_half(left, held, other, scale)


def own_kernel(left, held, own, *, scale):
    project_half(left, held, own, scale)


def back_sums(half, held):
    both = jnp.zeros((2 * K, held.shape[1]), jnp.float32)
    gram = jnp.zeros((3 * K, 3 * K), jnp.float32)
    for step in range(4):
        parts = split_bf16(half[:, span(step)])
        both += jnp.dot(
            jnp.concatenate(parts[:2], axis=0),
            held[span(step), :],
            preferred_element_type=jnp.float32,
        )
        gram += triple_gram(parts)
    return both[:K] + both[K:], fold_gram(gram)


def pack_gram(gram):
    blank = jnp.zeros((8, 128 - 2 * K), jnp.float32)
    return jnp.concatenate([gram[:8], gram[8:], blank], axis=1)


def unpack_gram(packed):
    return jnp.concatenate([packed[:, :K], packed[:, K : 2 * K]], axis=0)


def back_own_kernel(half, held, packed):
    back, gram = back_sums(half, held)
    tiles = held.shape[1] // 128
    for tile in range(tiles):
        packed[tile * K : (tile + 1) * K, :] = back[:, tile * 128 : (tile + 1) * 128]
    packed[tiles * K :, :] = pack_gram(gram)


def back_other_kernel(half, held, before, packed):
    back_own_kernel(half, held, packed)
    packed[...] = before[...] + packed[...]


def gram_kernel(half, packed):
    gram = jnp.zeros((3 * K, 3 * K), jnp.float32)
    for step in range(4):
        gram += triple_gram(split_bf16(half[:, span(step)]))
    packed[...] = pack_gram(fold_gram(gram))


def last_kernel(grams, half, basis, factor, *, scale):
    total = None
    for x in range(4):
        one, two, three, four = (grams[4 * x + k] for k in range(4))
        part = (one + three) + (two + four)
        total = part if total is None else total + part
    gram = unpack_gram(total)
    place = pl.multiple_of(lax.axis_index("y") * PIECE, PIECE)
    lower, ortho = eliminate(gram, half[:, pl.ds(place, PIECE)])
    basis[...] = ortho * scale
    factor[...] = lower.T[:K, :] / scale


def call(kernel, outs, *args, spaces=None, scratch=(), flops=0):
    whole = pl.BlockSpec(memory_space=pltpu.VMEM)
    return pl.pallas_call(
        kernel,
        in_specs=spaces or [whole] * len(args),
        out_specs=[whole] * len(outs),
        out_shape=[jax.ShapeDtypeStruct(*out) for out in outs],
        scratch_shapes=scratch,
        cost_estimate=pl.CostEstimate(
            flops=flops, bytes_accessed=flops // K, transcendentals=0
        ),
        compiler_params=pltpu.CompilerParams(vmem_limit_bytes=32 * 1024 * 1024),
    )(*args)


def body(affinity, seed_values, sku_ids):
    local_rows, local_columns = affinity.shape
    total_columns = local_columns * 8
    total_rows = local_rows * 32
    f32 = jnp.float32
    half_out = ((K, local_rows // 2), f32)
    left_out = ((K, local_columns), jnp.bfloat16)
    packed_out = ((local_columns // 128 * K + 8, 128), f32)
    pass_flops = K * local_rows * local_columns
    z = ("cube", "level")

    held_out = ((local_rows // 2, local_columns), jnp.bfloat16)
    far = pl.BlockSpec(memory_space=pltpu.HBM)
    affinity, seed_values, sku_ids = (
        pltpu.with_memory_space_constraint(value, pltpu.HBM)
        for value in (affinity, seed_values, sku_ids.reshape(1, -1))
    )

    left, held_other, held_own, other = call(
        functools.partial(first_kernel, columns=total_columns),
        [left_out, held_out, held_out, half_out],
        seed_values,
        sku_ids,
        affinity,
        spaces=[far, far, far],
        scratch=[
            pltpu.SMEM(seed_values.shape, jnp.int32),
            pltpu.VMEM(sku_ids.shape, jnp.int32),
            pltpu.SemaphoreType.DMA((2,)),
            pltpu.SemaphoreType.DMA((4,)),
            pltpu.SemaphoreType.DMA((4,)),
        ],
        flops=pass_flops,
    )
    scale = 1.0 / math.sqrt(total_columns)
    for repeat in range(ITERS + 1):
        arriving = swap(other, "core", 2, 1)
        own_scale = None if repeat == 0 else scale
        (own,) = call(
            functools.partial(own_kernel, scale=own_scale),
            [half_out],
            left,
            held_own,
            flops=pass_flops,
        )
        half = sum_four(own + arriving, "y", 4)
        if repeat < ITERS:
            sibling = swap(half, "core", 2, 1)
            (packed,) = call(back_own_kernel, [packed_out], half, held_own, flops=pass_flops)
            (packed,) = call(
                back_other_kernel, [packed_out], sibling, held_other, packed, flops=pass_flops
            )
            packed = sum_four(packed, "x", 4)
            packed = sum_four(packed, z, 8)
            left, other = call(
                functools.partial(solve_kernel, scale=scale),
                [left_out, half_out],
                packed,
                swap(packed, z, 8, 6),
                held_other,
                flops=pass_flops,
            )
        else:
            (gram,) = call(gram_kernel, [((8, 128), f32)], half)
            gram = sum_four(gram, z + ("core",), 16, (12, 1, 13))
            spread = jnp.broadcast_to(gram[None], (16,) + gram.shape)
            grams = lax.all_to_all(spread, ("x", "level"), 0, 0)
            basis, factor = call(
                functools.partial(last_kernel, scale=math.sqrt(total_rows)),
                [((K, PIECE), f32), ((K, K), f32)],
                grams,
                half,
            )
    return basis, factor


def solution(mesh):
    names = ("x", "cube", "level", "y", "core")
    split = Mesh(mesh.devices.reshape(4, 2, 4, 4, 2), names)
    row, col = names[:3], names[3:]
    return jax.shard_map(
        body,
        mesh=split,
        in_specs=(P(row, col), P(), P(col)),
        out_specs=(P(None, row + col), P()),
        check_vma=False,
    )
```

```python
import functools
import math

import jax
import jax.numpy as jnp
from jax import lax
from jax.experimental import pallas as pl
from jax.experimental.pallas import tpu as pltpu
from jax.sharding import Mesh, PartitionSpec as P

ITERS = 2
K = 16
PIECE = 512


mix_first = -2048144789
mix_second = -1028477387
golden = -1640531535
salt_value = 1540483477


def shifted(value, amount):
    return lax.shift_right_logical(value, jnp.full(value.shape, amount, jnp.int32))


def scramble(value):
    value = jnp.bitwise_xor(value, shifted(value, 16))
    value = value * jnp.int32(mix_first)
    value = jnp.bitwise_xor(value, shifted(value, 13))
    value = value * jnp.int32(mix_second)
    return jnp.bitwise_xor(value, shifted(value, 16))


def test_matrix(seeds, sku_ids, total_columns):
    first = scramble(jnp.bitwise_xor(seeds, sku_ids * jnp.int32(golden)))
    second = scramble(jnp.bitwise_xor(first, jnp.int32(salt_value)))
    uniform_a = (shifted(first, 9) + 1).astype(jnp.float32) / 8388608.0
    uniform_b = (shifted(second, 9) + 1).astype(jnp.float32) / 8388608.0
    gauss = jnp.sqrt(-2.0 * jnp.log(uniform_a)) * jnp.cos(6.283185307179586 * uniform_b)
    return (gauss / math.sqrt(total_columns)).astype(jnp.bfloat16)


def swap(value, axis, count, offset):
    return lax.ppermute(value, axis, [(i, i ^ offset) for i in range(count)])


def sum_four(value, axis, count, offsets=(2, 1, 3)):
    one, two, three = (swap(value, axis, count, k) for k in offsets)
    return (value + two) + (one + three)


def span(step):
    return slice(step * PIECE, (step + 1) * PIECE)


def project_piece(left, rows, scale):
    part = lax.dot_general(
        left, rows, (((1,), (1,)), ((), ())), preferred_element_type=jnp.float32
    )
    return part if scale is None else part * scale


def split_bf16(value):
    high = value.astype(jnp.bfloat16)
    rest = value - high.astype(jnp.float32)
    low = rest.astype(jnp.bfloat16)
    last = (rest - low.astype(jnp.float32)).astype(jnp.bfloat16)
    return high, low, last


def triple_gram(parts):
    stacked = jnp.concatenate(parts, axis=0)
    return lax.dot_general(
        stacked, stacked, (((1,), (1,)), ((), ())), preferred_element_type=jnp.float32
    )


def fold_gram(gram):
    rows = (gram[2 * K :] + gram[K : 2 * K]) + gram[:K]
    return (rows[:, 2 * K :] + rows[:, K : 2 * K]) + rows[:, :K]


def eliminate(gram, right):
    row = lax.broadcasted_iota(jnp.int32, (K, 128), 0)
    lane = lax.broadcasted_iota(jnp.int32, (K, 128), 1)
    columns = [jnp.broadcast_to(gram[:, k : k + 1], (K, 128)) for k in range(K)]
    lower = jnp.zeros((K, 128), jnp.float32)
    pivots = jnp.ones((K, 128), jnp.float32)
    for k in range(K):
        column = columns[k]
        pivot = jnp.broadcast_to(column[k : k + 1, :], (K, 128))
        factor = column * (1.0 / pivot)
        lower = jnp.where((lane == k) & (row >= k), column / jnp.sqrt(pivot), lower)
        pivots = jnp.where(row == k, pivot, pivots)
        factor = jnp.where(row > k, factor, 0.0)
        for j in range(k + 1, K):
            columns[j] = columns[j] - factor * jnp.broadcast_to(column[j : j + 1, :], (K, 128))
        wide = jnp.tile(factor, (1, right.shape[1] // 128))
        right = right - wide * right[k : k + 1, :]
    root = jnp.sqrt(pivots)
    return lower, right / jnp.tile(root, (1, right.shape[1] // 128))


def load_half(affinity, held, arrived, side):
    copies = []
    for step in range(4):
        place = pl.multiple_of((2 * step + side) * PIECE, PIECE)
        copies.append(
            pltpu.make_async_copy(
                affinity.at[pl.ds(place, PIECE)], held.at[span(step)], arrived.at[step]
            )
        )
        copies[-1].start()
    return copies


def project_half(left, held, target, scale, copies=None):
    for step in range(4):
        if copies is not None:
            copies[step].wait()
        target[:, span(step)] = project_piece(left[...], held[span(step), :], scale)


def first_kernel(
    seed_values,
    sku_ids,
    affinity,
    left,
    held_other,
    held_own,
    other,
    seeds_here,
    ids_here,
    small_arrived,
    other_arrived,
    own_arrived,
    *,
    columns,
):
    core = lax.axis_index("core")
    small = [
        pltpu.make_async_copy(seed_values, seeds_here, small_arrived.at[0]),
        pltpu.make_async_copy(sku_ids, ids_here, small_arrived.at[1]),
    ]
    for copy in small:
        copy.start()
    copies = load_half(affinity, held_other, other_arrived, 1 - core)
    for copy in small:
        copy.wait()
    row = lax.broadcasted_iota(jnp.int32, (K, 128), 0)
    seeds = jnp.zeros((K, 128), jnp.int32)
    for k in range(K):
        seeds = jnp.where(row == k, seeds_here[k], seeds)
    for start in range(0, ids_here.shape[1], 128):
        if start == ids_here.shape[1] // 2:
            later = load_half(affinity, held_own, own_arrived, core)
        ids = jnp.broadcast_to(ids_here[:, start : start + 128], (K, 128))
        left[:, start : start + 128] = test_matrix(seeds, ids, columns)
    project_half(left, held_other, other, None, copies)
    for copy in later:
        copy.wait()


def solve_kernel(mine, theirs, held, left, other, *, scale):
    total = mine[...] + theirs[...]
    tiles = held.shape[1] // 128
    back = jnp.concatenate([total[tile * K : (tile + 1) * K] for tile in range(tiles)], axis=1)
    _, back = eliminate(unpack_gram(total[tiles * K :]), back)
    left[...] = back.astype(jnp.bfloat16)
    project_half(left, held, other, scale)


def own_kernel(left, held, own, *, scale):
    project_half(left, held, own, scale)


def back_sums(half, held):
    both = jnp.zeros((2 * K, held.shape[1]), jnp.float32)
    gram = jnp.zeros((3 * K, 3 * K), jnp.float32)
    for step in range(4):
        parts = split_bf16(half[:, span(step)])
        both += jnp.dot(
            jnp.concatenate(parts[:2], axis=0),
            held[span(step), :],
            preferred_element_type=jnp.float32,
        )
        gram += triple_gram(parts)
    return both[:K] + both[K:], fold_gram(gram)


def pack_gram(gram):
    blank = jnp.zeros((8, 128 - 2 * K), jnp.float32)
    return jnp.concatenate([gram[:8], gram[8:], blank], axis=1)


def unpack_gram(packed):
    return jnp.concatenate([packed[:, :K], packed[:, K : 2 * K]], axis=0)


def back_own_kernel(half, held, packed):
    back, gram = back_sums(half, held)
    tiles = held.shape[1] // 128
    for tile in range(tiles):
        packed[tile * K : (tile + 1) * K, :] = back[:, tile * 128 : (tile + 1) * 128]
    packed[tiles * K :, :] = pack_gram(gram)


def back_other_kernel(half, held, before, packed):
    back_own_kernel(half, held, packed)
    packed[...] = before[...] + packed[...]


def gram_kernel(half, packed):
    gram = jnp.zeros((3 * K, 3 * K), jnp.float32)
    for step in range(4):
        gram += triple_gram(split_bf16(half[:, span(step)]))
    packed[...] = pack_gram(fold_gram(gram))


def last_kernel(grams, half, basis, factor, *, scale):
    total = None
    for x in range(4):
        one, two, three, four = (grams[4 * x + k] for k in range(4))
        part = (one + three) + (two + four)
        total = part if total is None else total + part
    gram = unpack_gram(total)
    place = pl.multiple_of(lax.axis_index("y") * PIECE, PIECE)
    lower, ortho = eliminate(gram, half[:, pl.ds(place, PIECE)])
    basis[...] = ortho * scale
    factor[...] = lower.T[:K, :] / scale


def call(kernel, outs, *args, spaces=None, scratch=(), flops=0):
    whole = pl.BlockSpec(memory_space=pltpu.VMEM)
    return pl.pallas_call(
        kernel,
        in_specs=spaces or [whole] * len(args),
        out_specs=[whole] * len(outs),
        out_shape=[jax.ShapeDtypeStruct(*out) for out in outs],
        scratch_shapes=scratch,
        cost_estimate=pl.CostEstimate(
            flops=flops, bytes_accessed=flops // K, transcendentals=0
        ),
        compiler_params=pltpu.CompilerParams(vmem_limit_bytes=32 * 1024 * 1024),
    )(*args)


def body(affinity, seed_values, sku_ids):
    local_rows, local_columns = affinity.shape
    total_columns = local_columns * 8
    total_rows = local_rows * 32
    f32 = jnp.float32
    half_out = ((K, local_rows // 2), f32)
    left_out = ((K, local_columns), jnp.bfloat16)
    packed_out = ((local_columns // 128 * K + 8, 128), f32)
    pass_flops = K * local_rows * local_columns
    z = ("cube", "level")

    held_out = ((local_rows // 2, local_columns), jnp.bfloat16)
    far = pl.BlockSpec(memory_space=pltpu.HBM)
    affinity, seed_values, sku_ids = (
        pltpu.with_memory_space_constraint(value, pltpu.HBM)
        for value in (affinity, seed_values, sku_ids.reshape(1, -1))
    )

    left, held_other, held_own, other = call(
        functools.partial(first_kernel, columns=total_columns),
        [left_out, held_out, held_out, half_out],
        seed_values,
        sku_ids,
        affinity,
        spaces=[far, far, far],
        scratch=[
            pltpu.SMEM(seed_values.shape, jnp.int32),
            pltpu.VMEM(sku_ids.shape, jnp.int32),
            pltpu.SemaphoreType.DMA((2,)),
            pltpu.SemaphoreType.DMA((4,)),
            pltpu.SemaphoreType.DMA((4,)),
        ],
        flops=pass_flops,
    )
    scale = 1.0 / math.sqrt(total_columns)
    for repeat in range(ITERS + 1):
        arriving = swap(other, "core", 2, 1)
        own_scale = None if repeat == 0 else scale
        (own,) = call(
            functools.partial(own_kernel, scale=own_scale),
            [half_out],
            left,
            held_own,
            flops=pass_flops,
        )
        half = sum_four(own + arriving, "y", 4)
        if repeat < ITERS:
            sibling = swap(half, "core", 2, 1)
            (packed,) = call(back_own_kernel, [packed_out], half, held_own, flops=pass_flops)
            (packed,) = call(
                back_other_kernel, [packed_out], sibling, held_other, packed, flops=pass_flops
            )
            packed = sum_four(packed, "x", 4)
            packed = sum_four(packed, z, 8)
            left, other = call(
                functools.partial(solve_kernel, scale=scale),
                [left_out, half_out],
                packed,
                swap(packed, z, 8, 6),
                held_other,
                flops=pass_flops,
            )
        else:
            (gram,) = call(gram_kernel, [((8, 128), f32)], half)
            gram = sum_four(gram, z + ("core",), 16, (12, 1, 13))
            spread = jnp.broadcast_to(gram[None], (16,) + gram.shape)
            grams = lax.all_to_all(spread, ("x", "level"), 0, 0)
            basis, factor = call(
                functools.partial(last_kernel, scale=math.sqrt(total_rows)),
                [((K, PIECE), f32), ((K, K), f32)],
                grams,
                half,
            )
    return basis, factor


def solution(mesh):
    names = ("x", "cube", "level", "y", "core")
    split = Mesh(mesh.devices.reshape(4, 2, 4, 4, 2), names)
    row, col = names[:3], names[3:]
    return jax.shard_map(
        body,
        mesh=split,
        in_specs=(P(row, col), P(), P(col)),
        out_specs=(P(None, row + col), P()),
        check_vma=False,
    )
```
